512 devices in a mesh: seq: 128 (over z_lo, x, y, core), head: 4 (over z_hi).
Axes of the slice: x: 4, y: 4, z: 16 (z_hi: 4, z_lo: 4; z = z_hi * 4 + z_lo), core: 2. Of those that a mesh axis runs over, the one named last changes fastest.
Arguments:
- queries: bfloat16 [16384, 1152], P('seq', 'head'), may hold values from -8 to 8
- key_heads: bfloat16 [16384, 1152], P('seq', 'head'), may hold values from -8 to 8
- value_heads: bfloat16 [16384, 1152], P('seq', 'head'), may hold values from -6 to 6
- out_grad: bfloat16 [16384, 1152], P('seq', 'head'), may hold values from -24 to 24
- out_proj: bfloat16 [1152, 1152], P(None, 'head'), may hold values from -0.1875 to 0.1875
- gate_scale: float32 [1, 1152], replicated, may hold values from 0.25 to 1.5
Outputs:
- query_grad: bfloat16 [16384, 1152], P('seq', 'head')
- key_grad: bfloat16 [16384, 1152], P('seq', 'head')
- value_grad: bfloat16 [16384, 1152], P('seq', 'head')
- proj_grad: float32 [1152, 1152], P('seq', 'head')
- gate_grad: float32 [1, 1152], replicated
The draws below stay inside these ranges and needn't reach their ends.
All inputs are finite; a program needn't handle non-finite values.
Results may differ from the reference program's by a relative error of at most 0.039.
Values may be sent and summed in bfloat16 or wider, within the bound.
A program may use at most 64 MiB of HBM per device.

```python
import math
import jax
import jax.numpy as jnp
from jax import lax

HEADS = 16
HEAD_DIM = 72
D = 1152
TF = 32
P_SIZE = 512
TOKENS = 16384


def draw_queries(key, part):
    key = jax.random.fold_in(key, 1)
    return jax.random.truncated_normal(key, -4.0, 4.0, (TOKENS, D), jnp.float32).astype(jnp.bfloat16)


def draw_key_heads(key, part):
    key = jax.random.fold_in(key, 2)
    return jax.random.truncated_normal(key, -4.0, 4.0, (TOKENS, D), jnp.float32).astype(jnp.bfloat16)


def with_spikes(values, stream_key, source, target, parts, factor):
    def block_of(axis_at):
        return (jnp.arange(values.shape[axis_at]) // (values.shape[axis_at] // parts)).reshape((-1,) + (1,) * (values.ndim - 1 - axis_at))

    first = jax.random.permutation(stream_key, parts)[block_of(target)]
    far = (block_of(target) + parts // 2) % parts
    return jnp.where((block_of(source) == first) | (block_of(source) == far), factor * values, values)


def levels(stream_key, dims, cuts, smallest, largest):
    def one(axis_at, blocks):
        draws = jax.random.uniform(jax.random.fold_in(jax.random.fold_in(stream_key, 6), axis_at), (blocks,), jnp.float32, smallest / len(cuts), largest / len(cuts))
        return jnp.repeat(jnp.exp(draws), dims[axis_at] // blocks).reshape((-1,) + (1,) * (len(dims) - axis_at - 1))

    factor_of = one(*cuts[0])
    for cut in cuts[1:]:
        factor_of = factor_of * one(*cut)
    return factor_of


def centred(rng, extent, deviation, limit, pieces=(), held_as=jnp.bfloat16):
    loudness = levels(rng, extent, pieces, -0.22, 0.18) if pieces else 1.0
    array = jax.random.normal(rng, extent, jnp.float32) * deviation * loudness
    return jnp.minimum(jnp.maximum(array, -limit), limit).astype(held_as)


def gaussian_with(stream_key, dims, scale, bound, cuts, heavy, held_as=jnp.bfloat16):
    array = scale * jax.random.normal(stream_key, dims, jnp.float32)
    if cuts:
        array = array * levels(stream_key, dims, cuts, -0.22, 0.18)
    return jnp.clip(with_spikes(array, jax.random.fold_in(stream_key, 3), *heavy), -bound, bound).astype(held_as)


def setup_inputs(seed: int = 0) -> dict:
    key_list = jax.random.split(jax.random.key(seed), 7)
    return {
        "queries": draw_queries(jax.random.fold_in(key_list[6], 71), 0),
        "key_heads": draw_key_heads(jax.random.fold_in(key_list[6], 71), 0),
        "value_heads": centred(key_list[2], (TOKENS, D), 1.0, 6.0, ((0, 128), (1, 4))),
        "out_grad": gaussian_with(key_list[3], (TOKENS, D), 1.0, 24.0, ((0, 128), (1, 4)), (0, 1, 128, 5.5)),
        "out_proj": centred(key_list[4], (D, D), D ** -0.5, 0.1875, ((1, 4),)),
        "gate_scale": jnp.clip(jax.random.uniform(key_list[5], (1, D), jnp.float32, 0.25, 1.5), 0.25, 1.5),
    }


def rounded(x):
    return lax.optimization_barrier(x.astype(jnp.bfloat16))

def reference(queries, key_heads, value_heads, out_grad, out_proj, gate_scale):
    scale = HEAD_DIM ** (-0.5)
    grad_scale = 1.0 / math.sqrt(TF * P_SIZE)

    def split(x):
        return x.astype(jnp.float32).reshape(TF, P_SIZE, HEADS, HEAD_DIM)

    def clip_step(carry, inputs):
        q_clip, k_clip, v_clip, dy_clip, gate_row = inputs
        upstream = dy_clip.astype(jnp.float32)
        scaled = rounded(upstream * gate_row[None, :])
        attn_grad = rounded(jnp.dot(scaled, out_proj, preferred_element_type=jnp.float32))
        scores = jnp.einsum('fxhd,gxhd->xhfg', split(q_clip), split(k_clip)) * scale
        top = lax.optimization_barrier(jnp.max(scores, axis=-1, keepdims=True))
        expo = jnp.exp(scores - top)
        probs = expo / lax.optimization_barrier(jnp.sum(expo, axis=-1, keepdims=True))
        light = rounded(probs)
        attn_out = rounded(jnp.einsum('xhfg,gxhd->fxhd', light.astype(jnp.float32), split(v_clip)))
        out_rows = attn_out.reshape(TF * P_SIZE, D)
        delta = lax.optimization_barrier(jnp.sum(split(attn_grad) * split(out_rows), axis=-1))
        dprob = jnp.einsum('fxhd,gxhd->xhfg', split(attn_grad), split(v_clip))
        dscore = probs * (dprob - jnp.transpose(delta, (1, 2, 0))[..., None])
        dlight = rounded(dscore).astype(jnp.float32)
        dq = (jnp.einsum('xhfg,gxhd->fxhd', dlight, split(k_clip)) * scale).astype(jnp.bfloat16)
        dk = (jnp.einsum('xhfg,fxhd->gxhd', dlight, split(q_clip)) * scale).astype(jnp.bfloat16)
        dv = jnp.einsum('xhfg,fxhd->gxhd', light.astype(jnp.float32), split(attn_grad)).astype(jnp.bfloat16)
        proj_term = lax.dot_general(scaled, out_rows, (((0,), (0,)), ((), ())), preferred_element_type=jnp.float32)
        produced = jnp.dot(out_rows, out_proj.T, preferred_element_type=jnp.float32)
        gate_part = lax.optimization_barrier(jnp.sum(upstream * produced, axis=0))
        return (carry + proj_term, (dq.reshape(TF * P_SIZE, D), dk.reshape(TF * P_SIZE, D), dv.reshape(TF * P_SIZE, D), gate_part))
    clips = gate_scale.shape[0]
    stacked = (queries.reshape(clips, TF * P_SIZE, D), key_heads.reshape(clips, TF * P_SIZE, D), value_heads.reshape(clips, TF * P_SIZE, D), out_grad.reshape(clips, TF * P_SIZE, D), gate_scale)
    initial = jnp.zeros((D, D), jnp.float32)
    proj_sum, (dq_all, dk_all, dv_all, gate_parts) = lax.scan(clip_step, initial, stacked)
    total = clips * TF * P_SIZE
    return (dq_all.reshape(total, D), dk_all.reshape(total, D), dv_all.reshape(total, D), proj_sum * grad_scale, gate_parts * grad_scale)
```

```python
import math

import jax
import jax.numpy as jnp
from jax import lax
from jax.experimental import pallas as pl
from jax.experimental.pallas import tpu as pltpu
from jax.sharding import PartitionSpec as P

MESH = pl.DeviceIdType.MESH
BF = jnp.bfloat16
F32 = jnp.float32
HEAD_DIM = 72
TF = 32
P_SIZE = 512
W = 288
N = 128
SCALE = HEAD_DIM ** (-0.5)
GRAD_SCALE = 1.0 / math.sqrt(TF * P_SIZE)


def iota(shape, dim):
    return lax.broadcasted_iota(jnp.int32, shape, dim)


def onehot(cond):
    return jnp.where(cond, 1.0, 0.0).astype(BF)


def mm(a, b):
    return jnp.dot(a, b, preferred_element_type=F32)


def mm_nt(a, b):
    return lax.dot_general(a, b, (((1,), (1,)), ((), ())), preferred_element_type=F32)


def mm_tn(a, b):
    return lax.dot_general(a, b, (((0,), (0,)), ((), ())), preferred_element_type=F32)


def kernel(
    q_hbm, k_hbm, v_hbm, g_hbm, w_hbm, s_hbm,
    dq_ref, dk_ref, dv_ref, proj_ref, gate_ref,
    q_in, k_in, v_in, g_in, w_in, s_in,
    send, recv, back, home,
    og_main, og_tail, rs, c_recv, plane_send, plane_recv,
    z_send, z_recv, h_all,
    in_sem, s_sem, r_sem,
):
    i = lax.axis_index("seq")
    h = lax.axis_index("head")
    f = i // 4
    r = i % 4
    core = i % 2
    y = (i // 2) % 4
    x = (i // 8) % 4
    z = i // 32
    xy = x * 4 + y

    loads = []
    for n, (src, dst) in enumerate(
        ((q_hbm, q_in), (k_hbm, k_in), (v_hbm, v_in), (g_hbm, g_in), (w_hbm, w_in), (s_hbm, s_in))
    ):
        copy = pltpu.make_async_copy(src, dst, in_sem.at[n])
        copy.start()
        loads.append(copy)

    barrier = pltpu.get_barrier_semaphore()

    def greet(seq, head):
        pl.semaphore_signal(barrier, inc=1, device_id=(seq, head), device_id_type=MESH)

    def greet_frames(t, carry):
        greet(4 * ((f + t) % 32) + r, h)
        return carry

    lax.fori_loop(1, 32, greet_frames, 0)

    def greet_plane(t, carry):
        greet(((z * 4 + t // 2) * 4 + 2 * (t % 2) + 1 - y % 2) * 2 + core, h)
        return carry

    lax.fori_loop(0, 8, greet_plane, 0)
    greet(i + 1 - 2 * core, h)
    for t in range(1, 4):
        greet(i, (h + t) % 4)

    row, col = iota((N, N), 0), iota((N, N), 1)
    perm = onehot(col == (row % 16) // 4 * 32 + row // 16 * 4 + row % 4)
    perm_t = onehot(row == (col % 16) // 4 * 32 + col // 16 * 4 + col % 4)
    prow, pcol = iota((W, N), 0), iota((W, N), 1)
    place = [onehot(jnp.logical_and(pcol // 32 == k, prow == 256 + pcol - 32 * k)) for k in range(4)]
    urow, ucol = iota((N, 32), 0), iota((N, 32), 1)
    unplace = [onehot(urow == 32 * k + ucol) for k in range(4)]

    for copy in loads[:4]:
        copy.wait()

    for g in range(4):
        rows = slice(32 * g, 32 * g + 32)
        stack = jnp.concatenate([q_in[rows], k_in[rows], v_in[rows], g_in[rows]], axis=0)
        send[8 * g : 8 * g + 8] = mm(perm, stack).astype(BF).reshape(8, 16, W)

    pl.semaphore_wait(barrier, 43)

    def scatter(src, dst, n):
        own = pltpu.make_async_copy(src.at[f], dst.at[f], r_sem.at[n])
        own.start()

        def one(t, carry):
            j = (f + t) % 32
            pltpu.make_async_remote_copy(
                src.at[j], dst.at[f], s_sem.at[n], r_sem.at[n],
                device_id=(4 * j + r, h), device_id_type=MESH,
            ).start()
            return carry

        lax.fori_loop(1, 32, one, 0)

    def wait_all(ref, sem):
        pltpu.make_async_copy(ref, ref, sem).wait()

    scatter(send, recv, 0)

    heads = [onehot(iota((1, W), 1) // HEAD_DIM == k) for k in range(4)]
    same = iota((N, N), 0) % 4 == iota((N, N), 1) % 4
    drow, dcol = iota((512, W), 0), iota((512, W), 1)
    blk, kk = drow // 16, drow % 16
    spread = onehot(
        jnp.logical_and(kk < 9, dcol == (blk % 16) * 18 + blk // 16 * 9 + kk)
    )

    wait_all(recv, r_sem.at[0])

    parts = [mm(perm_t, recv[8 * g : 8 * g + 8].reshape(N, W)).astype(BF) for g in range(4)]
    q, k, v, og = (
        jnp.concatenate([p[32 * a : 32 * a + 32] for p in parts], axis=0) for a in range(4)
    )

    og_main[h] = og[:, :256]
    tail = mm(og[0:32], place[0])
    for n in range(1, 4):
        tail += mm(og[32 * n : 32 * n + 32], place[n])
    og_tail[h] = tail.astype(BF)
    gathers = []
    for t in range(1, 4):
        peer = (h + t) % 4
        for n, ref in ((0, og_main), (1, og_tail)):
            copy = pltpu.make_async_remote_copy(
                ref.at[h], ref.at[h], s_sem.at[4 + 2 * t + n], r_sem.at[4 + 2 * t + n],
                device_id=(i, peer), device_id_type=MESH,
            )
            copy.start()
            gathers.append(copy)

    km = jnp.concatenate([k * m for m in heads], axis=0)
    vm = jnp.concatenate([v * m for m in heads], axis=0)
    scores = mm_nt(q, km) * SCALE
    probs = []
    for n in range(4):
        sc = jnp.where(same, scores[:, N * n : N * n + N], -1e30)
        e = jnp.where(same, jnp.exp(sc - jnp.max(sc, axis=-1, keepdims=True)), 0.0)
        probs.append(e / jnp.sum(e, axis=-1, keepdims=True))
    light = [p.astype(BF) for p in probs]
    out = mm(jnp.concatenate(light, axis=1), vm).astype(BF)

    loads[4].wait()
    loads[5].wait()
    for copy in gathers:
        copy.wait()

    do = jnp.zeros((N, W), F32)
    tail_acc = jnp.zeros((512, N), F32)
    gate_rows = []
    for n in range(4):
        packed = og_tail[n]
        t32 = jnp.concatenate([mm(packed, unplace[a]) for a in range(4)], axis=0)
        up = jnp.concatenate([og_main[n].astype(F32), t32], axis=1)
        scaled = (up * s_in[:, W * n : W * n + W]).astype(BF)
        wn = w_in[W * n : W * n + W, :]
        do += mm(scaled, wn)
        produced = mm_nt(out, wn)
        gate_rows.append(jnp.sum(up * produced, axis=0, keepdims=True))
        scaled_t = mm_nt(spread, scaled).astype(BF)
        main = mm(scaled_t, out[:, :256])
        rs[:, :, 256 * n : 256 * n + 256] = main.astype(BF).reshape(2, 256, 256)
        tail_acc += mm(scaled_t, mm(out, place[n]).astype(BF))
    rs[:, :, 1024:1152] = tail_acc.astype(BF).reshape(2, 256, N)
    gate_row = jnp.concatenate(gate_rows, axis=1)
    is_gate = iota((512, 1), 0) % 16 == 9
    rs[...] = jnp.where(is_gate, gate_row, rs[...].reshape(512, 1152).astype(F32)).astype(BF).reshape(2, 256, 1152)

    pair = pltpu.make_async_remote_copy(
        rs.at[1 - core], c_recv, s_sem.at[1], r_sem.at[1],
        device_id=(i + 1 - 2 * core, h), device_id_type=MESH,
    )
    pair.start()

    do = do.astype(BF)
    dprob = mm_nt(do, vm)
    dlight = []
    for n in range(4):
        dp = dprob[:, N * n : N * n + N]
        delta = jnp.sum(light[n].astype(F32) * dp, axis=-1, keepdims=True)
        dlight.append((probs[n] * (dp - delta)).astype(BF))
    dq = (mm(jnp.concatenate(dlight, axis=1), km) * SCALE).astype(BF)
    qm = jnp.concatenate([q * m for m in heads], axis=0)
    dom = jnp.concatenate([do * m for m in heads], axis=0)
    dk = (mm_tn(jnp.concatenate(dlight, axis=0), qm) * SCALE).astype(BF)
    dv = mm_tn(jnp.concatenate(light, axis=0), dom).astype(BF)
    zero = jnp.zeros((32, W), BF)
    for g in range(4):
        rows = slice(32 * g, 32 * g + 32)
        stack = jnp.concatenate([dq[rows], dk[rows], dv[rows], zero], axis=0)
        back[8 * g : 8 * g + 8] = mm(perm, stack).astype(BF).reshape(8, 16, W)
    scatter(back, home, 2)

    pair.wait()
    plane_send[...] = (
        (rs[core].astype(F32) + c_recv[...].astype(F32)).astype(BF).reshape(16, 16, 1152)
    )
    own = pltpu.make_async_copy(plane_send.at[xy], plane_recv.at[xy], r_sem.at[3])
    own.start()

    def to_plane(t, carry):
        j = (xy + t) % 16
        pltpu.make_async_remote_copy(
            plane_send.at[j], plane_recv.at[xy], s_sem.at[3], r_sem.at[3],
            device_id=((z * 16 + j) * 2 + core, h), device_id_type=MESH,
        ).start()
        return carry

    lax.fori_loop(1, 16, to_plane, 0)
    wait_all(plane_recv, r_sem.at[3])
    total = plane_recv[0].astype(F32)
    for n in range(1, 16):
        total += plane_recv[n].astype(F32)
    zrow = iota((16, 384), 0)
    tail = total[:, 1024:1152].astype(BF)
    for n in range(4):
        t32 = mm(tail, onehot(jnp.logical_and(iota((N, N), 0) == 32 * n + iota((N, N), 1), iota((N, N), 1) < 32)))
        msg = jnp.concatenate([total[:, 256 * n : 256 * n + 256], t32], axis=1)
        for j in range(3):
            msg = jnp.where(zrow == 9 + j, total[9:10, 384 * j : 384 * j + 384], msg)
        z_send[n] = msg.astype(BF)
    own = pltpu.make_async_copy(z_send.at[z], z_recv.at[z], r_sem.at[4])
    own.start()
    for t in range(1, 4):
        j = (z + t) % 4
        pltpu.make_async_remote_copy(
            z_send.at[j], z_recv.at[z], s_sem.at[4], r_sem.at[4],
            device_id=(j * 32 + i % 32, h), device_id_type=MESH,
        ).start()
    wait_all(z_recv, r_sem.at[4])
    total = z_recv[0].astype(F32)
    for n in range(1, 4):
        total += z_recv[n].astype(F32)
    proj_ref[...] = total[0:9, 0:W] * GRAD_SCALE
    h_all[h] = total[8:16]
    sums = []
    for t in range(1, 4):
        copy = pltpu.make_async_remote_copy(
            h_all.at[h], h_all.at[h], s_sem.at[11 + t], r_sem.at[11 + t],
            device_id=(i, (h + t) % 4), device_id_type=MESH,
        )
        copy.start()
        sums.append(copy)

    wait_all(home, r_sem.at[2])
    parts = [mm(perm_t, home[8 * g : 8 * g + 8].reshape(N, W)).astype(BF) for g in range(4)]
    for a, ref in enumerate((dq_ref, dk_ref, dv_ref)):
        for g in range(4):
            ref[32 * g : 32 * g + 32, :] = parts[g][32 * a : 32 * a + 32]

    for copy in sums:
        copy.wait()
    total = h_all[0] + h_all[1] + h_all[2] + h_all[3]
    for j in range(3):
        gate_ref[:, 384 * j : 384 * j + 384] = total[1 + j : 2 + j] * GRAD_SCALE

    wait_all(send.at[pl.ds(0, 31)], s_sem.at[0])
    wait_all(back.at[pl.ds(0, 31)], s_sem.at[2])
    wait_all(plane_send.at[pl.ds(0, 15)], s_sem.at[3])
    wait_all(z_send.at[pl.ds(0, 3)], s_sem.at[4])


def body(queries, key_heads, value_heads, out_grad, out_proj, gate_scale):
    anyspace = pl.BlockSpec(memory_space=pl.ANY)
    vmem = pl.BlockSpec(memory_space=pltpu.VMEM)
    token = pltpu.VMEM((N, W), BF)
    frames = pltpu.VMEM((32, 16, W), BF)
    return pl.pallas_call(
        kernel,
        out_shape=(
            jax.ShapeDtypeStruct((N, W), BF),
            jax.ShapeDtypeStruct((N, W), BF),
            jax.ShapeDtypeStruct((N, W), BF),
            jax.ShapeDtypeStruct((9, W), F32),
            jax.ShapeDtypeStruct((1, 1152), F32),
        ),
        in_specs=[anyspace] * 6,
        out_specs=(vmem,) * 5,
        scratch_shapes=[
            token, token, token, token,
            pltpu.VMEM((1152, W), BF),
            pltpu.VMEM((1, 1152), F32),
            frames, frames, frames, frames,
            pltpu.VMEM((4, N, 256), BF),
            pltpu.VMEM((4, 32, N), BF),
            pltpu.VMEM((2, 256, 1152), BF),
            pltpu.VMEM((256, 1152), BF),
            pltpu.VMEM((16, 16, 1152), BF),
            pltpu.VMEM((16, 16, 1152), BF),
            pltpu.VMEM((4, 16, 384), BF),
            pltpu.VMEM((4, 16, 384), BF),
            pltpu.VMEM((4, 8, 384), F32),
            pltpu.SemaphoreType.DMA((6,)),
            pltpu.SemaphoreType.DMA((15,)),
            pltpu.SemaphoreType.DMA((15,)),
        ],
        compiler_params=pltpu.CompilerParams(
            collective_id=0, has_side_effects=True, vmem_limit_bytes=40 * 1024 * 1024
        ),
    )(queries, key_heads, value_heads, out_grad, out_proj, gate_scale)


def solution(mesh):
    placed = (
        P("seq", "head"),
        P("seq", "head"),
        P("seq", "head"),
        P("seq", "head"),
        P(None, "head"),
        P(),
    )
    return jax.shard_map(
        body,
        mesh=mesh,
        in_specs=placed,
        out_specs=(P("seq", "head"), P("seq", "head"), P("seq", "head"), P("seq", "head"), P()),
        check_vma=False,
    )
```

```python
import math

import jax
import jax.numpy as jnp
from jax import lax
from jax.experimental import pallas as pl
from jax.experimental.pallas import tpu as pltpu
from jax.sharding import PartitionSpec as P

MESH = pl.DeviceIdType.MESH
BF = jnp.bfloat16
F32 = jnp.float32
HEAD_DIM = 72
TF = 32
P_SIZE = 512
W = 288
N = 128
SCALE = HEAD_DIM ** (-0.5)
GRAD_SCALE = 1.0 / math.sqrt(TF * P_SIZE)


def iota(shape, dim):
    return lax.broadcasted_iota(jnp.int32, shape, dim)


def onehot(cond):
    return jnp.where(cond, 1.0, 0.0).astype(BF)


def mm(a, b):
    return jnp.dot(a, b, preferred_element_type=F32)


def mm_nt(a, b):
    return lax.dot_general(a, b, (((1,), (1,)), ((), ())), preferred_element_type=F32)


def mm_tn(a, b):
    return lax.dot_general(a, b, (((0,), (0,)), ((), ())), preferred_element_type=F32)


def masks():
    own = onehot(iota((N, N), 1) // 32 == iota((N, N), 0) % 4)
    fold = onehot(iota((N, 32), 0) % 32 == iota((N, 32), 1))
    return own, fold


def target(c, n, rows):
    b, j, p = c // 32, (c % 32) // 4, c % 4
    return j * rows + jnp.where(b < 2 * n, 4 * b + p, 6 * n + b)


def pack(arrays, rows, own, fold, dst):
    n = len(arrays)
    sel = onehot(iota((8 * rows, 288 * n // 3), 0) == target(iota((1, 288 * n // 3), 1), n, rows))
    tails = [lax.dot_general(x[:, 256:W], fold, (((1,), (1,)), ((), ())), preferred_element_type=F32).astype(BF) * own for x in arrays]
    for g in range(4):
        at = slice(32 * g, 32 * g + 32)
        stack = [x[at, N * t : N * t + N] for x in arrays for t in range(2)] + [x[at] for x in tails]
        dst[8 * g : 8 * g + 8] = mm(sel, jnp.concatenate(stack, axis=0)).astype(BF).reshape(8, rows, N)


def unpack(src, n, rows, own, fold):
    sel = onehot(iota((288 * n // 3, 8 * rows), 1) == target(iota((288 * n // 3, 1), 0), n, rows))
    parts = [mm(sel, src[8 * g : 8 * g + 8].reshape(8 * rows, N)).astype(BF) for g in range(4)]

    def tile(b):
        return jnp.concatenate([p[32 * b : 32 * b + 32] for p in parts], axis=0)

    return [
        jnp.concatenate([tile(2 * a), tile(2 * a + 1), mm(tile(2 * n + a) * own, fold).astype(BF)], axis=1)
        for a in range(n)
    ]


def kernel(
    q_hbm, k_hbm, v_hbm, g_hbm, w_hbm, s_hbm,
    home, proj_out, h_all,
    q_in, k_in, v_in, g_in, w_in, s_in,
    g_send, g_recv, send, recv, back,
    og_all, rs, c_recv, plane_send, plane_recv,
    z_send, z_recv, z_sum,
    in_sem, s_sem, r_sem,
):
    i = lax.axis_index("seq")
    h = lax.axis_index("head")
    f = i // 4
    r = i % 4
    core = i % 2
    y = (i // 2) % 4
    x = (i // 8) % 4
    z = i // 32
    xy = x * 4 + y

    loads = []
    for n, (src, dst) in enumerate(
        ((g_hbm, g_in), (q_hbm, q_in), (k_hbm, k_in), (v_hbm, v_in), (w_hbm, w_in), (s_hbm, s_in))
    ):
        copy = pltpu.make_async_copy(src, dst, in_sem.at[n])
        copy.start()
        loads.append(copy)

    barrier = pltpu.get_barrier_semaphore()

    def greet(seq, head):
        pl.semaphore_signal(barrier, inc=1, device_id=(seq, head), device_id_type=MESH)

    for t in range(1, 4):
        greet(i, (h + t) % 4)

    def greet_frames(t, carry):
        greet(4 * ((f + t) % 32) + r, h)
        return carry

    lax.fori_loop(1, 32, greet_frames, 0)

    def greet_plane(t, carry):
        greet(((z * 4 + t // 2) * 4 + 2 * (t % 2) + 1 - y % 2) * 2 + core, h)
        return carry

    lax.fori_loop(0, 8, greet_plane, 0)
    greet(i + 1 - 2 * core, h)

    own, fold = masks()
    eye = onehot(iota((N, N), 0) == iota((N, N), 1))

    def scatter(src, dst, n):
        pltpu.make_async_copy(src.at[f], dst.at[f], r_sem.at[n]).start()

        def one(t, carry):
            j = (f + t) % 32
            pltpu.make_async_remote_copy(
                src.at[j], dst.at[f], s_sem.at[n], r_sem.at[n],
                device_id=(4 * j + r, h), device_id_type=MESH,
            ).start()
            return carry

        lax.fori_loop(1, 32, one, 0)

    def wait_all(ref, sem):
        pltpu.make_async_copy(ref, ref, sem).wait()

    loads[0].wait()
    pack([mm_nt(eye, g_in[...]).astype(BF)], 16, own, fold, g_send)
    pl.semaphore_wait(barrier, 43)
    scatter(g_send, g_recv, 14)
    for copy in loads[1:4]:
        copy.wait()
    pack([mm_nt(eye, ref[...]).astype(BF) for ref in (q_in, k_in, v_in)], 32, own, fold, send)
    scatter(send, recv, 0)

    heads = [onehot(iota((1, W), 1) // HEAD_DIM == k) for k in range(4)]
    same = iota((N, N), 0) % 4 == iota((N, N), 1) % 4
    drow, dcol = iota((512, W), 0), iota((512, W), 1)
    blk, kk = drow // 16, drow % 16
    spread = onehot(jnp.logical_and(kk < 9, dcol == (blk % 16) * 18 + blk // 16 * 9 + kk))
    crow, ccol = iota((72, N), 0), iota((72, N), 1)
    squeeze = onehot(
        ccol == jnp.where(crow < 64, (crow % 32) // 4 * 16 + crow // 32 * 4 + crow % 4, (crow - 64) * 16 + 8)
    )
    repeat = onehot(iota((N, 32), 0) // 4 == iota((N, 32), 1))
    prow, pcol = iota((W, N), 0), iota((W, N), 1)
    place = [onehot(jnp.logical_and(pcol // 32 == k, prow == 256 + pcol - 32 * k)) for k in range(4)]

    wait_all(g_recv, r_sem.at[14])
    parts = [mm(squeeze, g_recv[8 * g : 8 * g + 8].reshape(N, N)).astype(BF) for g in range(4)]
    og_all[h] = jnp.concatenate(
        [p[0:32] for p in parts] + [p[32:64] for p in parts]
        + [jnp.concatenate([p[64:72] for p in parts], axis=0)],
        axis=0,
    )

    right, left = (h + 1) % 4, (h + 3) % 4
    first, second = pl.ds(0, 144), pl.ds(144, 144)

    def pass_on(slot, rows, peer, n):
        return pltpu.make_async_remote_copy(
            og_all.at[slot, rows], og_all.at[slot, rows], s_sem.at[n], r_sem.at[n],
            device_id=(i, peer), device_id_type=MESH,
        )

    ring = [
        pass_on(h, first, right, 5), pass_on(h, second, left, 6),
        pass_on(h, second, right, 7), pass_on(h, first, left, 8),
    ]
    for copy in ring:
        copy.start()

    wait_all(recv, r_sem.at[0])
    q, k, v = unpack(recv, 3, 32, own, fold)
    km = jnp.concatenate([k * m for m in heads], axis=0)
    vm = jnp.concatenate([v * m for m in heads], axis=0)
    scores = mm_nt(q, km) * SCALE
    probs = []
    for n in range(4):
        sc = jnp.where(same, scores[:, N * n : N * n + N], -1e30)
        e = jnp.where(same, jnp.exp(sc - jnp.max(sc, axis=-1, keepdims=True)), 0.0)
        probs.append(e / jnp.sum(e, axis=-1, keepdims=True))
    light = [p.astype(BF) for p in probs]
    out = mm(jnp.concatenate(light, axis=1), vm).astype(BF)

    ring[0].wait_recv()
    far = [pass_on(left, first, right, 9)]
    far[0].start()
    ring[1].wait_recv()
    far.append(pass_on(right, second, left, 10))
    far[1].start()
    loads[4].wait()
    loads[5].wait()
    ring[2].wait_recv()
    ring[3].wait_recv()
    for copy in far:
        copy.wait_recv()

    do = jnp.zeros((N, W), F32)
    tail_acc = jnp.zeros((512, N), F32)
    gate_rows = []
    for n in range(4):
        tail = mm(mm(repeat, og_all[n, 256:288]).astype(BF) * own, fold)
        up = jnp.concatenate([og_all[n, 0:128].astype(F32), og_all[n, 128:256].astype(F32), tail], axis=1)
        scaled = (up * s_in[:, W * n : W * n + W]).astype(BF)
        wn = w_in[:, W * n : W * n + W]
        do += mm_nt(scaled, wn)
        produced = mm(out, wn)
        gate_rows.append(jnp.sum(up * produced, axis=0, keepdims=True))
        scaled_t = mm_nt(spread, scaled).astype(BF)
        main = mm(scaled_t, out[:, :256])
        rs[:, :, 256 * n : 256 * n + 256] = main.astype(BF).reshape(2, 256, 256)
        tail_acc += mm(scaled_t, mm(out, place[n]).astype(BF))
    rs[:, :, 1024:1152] = tail_acc.astype(BF).reshape(2, 256, N)
    gate_row = jnp.concatenate(gate_rows, axis=1)
    is_gate = iota((512, 1), 0) % 16 == 9
    rs[...] = jnp.where(is_gate, gate_row, rs[...].reshape(512, 1152).astype(F32)).astype(BF).reshape(2, 256, 1152)

    pair = pltpu.make_async_remote_copy(
        rs.at[1 - core], c_recv, s_sem.at[1], r_sem.at[1],
        device_id=(i + 1 - 2 * core, h), device_id_type=MESH,
    )
    pair.start()

    do = do.astype(BF)
    dprob = mm_nt(do, vm)
    dlight = []
    for n in range(4):
        dp = dprob[:, N * n : N * n + N]
        delta = jnp.sum(light[n].astype(F32) * dp, axis=-1, keepdims=True)
        dlight.append((probs[n] * (dp - delta)).astype(BF))
    dq = (mm(jnp.concatenate(dlight, axis=1), km) * SCALE).astype(BF)
    qm = jnp.concatenate([q * m for m in heads], axis=0)
    dom = jnp.concatenate([do * m for m in heads], axis=0)
    dk = (mm_tn(jnp.concatenate(dlight, axis=0), qm) * SCALE).astype(BF)
    dv = mm_tn(jnp.concatenate(light, axis=0), dom).astype(BF)
    pack([dq, dk, dv], 32, own, fold, back)
    scatter(back, home, 2)

    pair.wait()
    plane_send[...] = (
        (rs[core].astype(F32) + c_recv[...].astype(F32)).astype(BF).reshape(16, 16, 1152)
    )
    pltpu.make_async_copy(plane_send.at[xy], plane_recv.at[xy], r_sem.at[3]).start()

    def to_plane(t, carry):
        j = (xy + t) % 16
        pltpu.make_async_remote_copy(
            plane_send.at[j], plane_recv.at[xy], s_sem.at[3], r_sem.at[3],
            device_id=((z * 16 + j) * 2 + core, h), device_id_type=MESH,
        ).start()
        return carry

    lax.fori_loop(1, 16, to_plane, 0)
    wait_all(plane_recv, r_sem.at[3])
    total = plane_recv[0].astype(F32)
    for n in range(1, 16):
        total += plane_recv[n].astype(F32)
    zrow = iota((16, 384), 0)
    tail = total[:, 1024:1152].astype(BF)
    for n in range(4):
        t32 = mm(tail, onehot(jnp.logical_and(iota((N, N), 0) == 32 * n + iota((N, N), 1), iota((N, N), 1) < 32)))
        msg = jnp.concatenate([total[:, 256 * n : 256 * n + 256], t32], axis=1)
        for j in range(3):
            msg = jnp.where(zrow == 9 + j, total[9:10, 384 * j : 384 * j + 384], msg)
        z_send[n] = msg.astype(BF)
    pltpu.make_async_copy(z_send.at[z], z_recv.at[z], r_sem.at[4]).start()
    for t in range(1, 4):
        j = (z + t) % 4
        pltpu.make_async_remote_copy(
            z_send.at[j], z_recv.at[z], s_sem.at[4], r_sem.at[4],
            device_id=(j * 32 + i % 32, h), device_id_type=MESH,
        ).start()
    wait_all(z_recv, r_sem.at[4])
    total = z_recv[0].astype(F32)
    for n in range(1, 4):
        total += z_recv[n].astype(F32)
    z_sum[...] = total
    stores = [
        pltpu.make_async_copy(z_sum, proj_out, in_sem.at[6]),
        pltpu.make_async_copy(z_sum.at[pl.ds(8, 8)], h_all.at[h], in_sem.at[7]),
    ]
    for t in range(1, 4):
        stores.append(pltpu.make_async_remote_copy(
            z_sum.at[pl.ds(8, 8)], h_all.at[h], s_sem.at[10 + t], r_sem.at[10 + t],
            device_id=(i, (h + t) % 4), device_id_type=MESH,
        ))
    for copy in stores:
        copy.start()

    for copy in ring + far:
        copy.wait_send()
    wait_all(g_send.at[pl.ds(0, 31)], s_sem.at[14])
    wait_all(send.at[pl.ds(0, 31)], s_sem.at[0])
    wait_all(back.at[pl.ds(0, 31)], s_sem.at[2])
    wait_all(plane_send.at[pl.ds(0, 15)], s_sem.at[3])
    wait_all(z_send.at[pl.ds(0, 3)], s_sem.at[4])
    wait_all(back, r_sem.at[2])
    for copy in stores:
        copy.wait()


def finish(home, proj_in, h_in, dq_ref, dk_ref, dv_ref, proj_ref, gate_ref):
    own, fold = masks()
    eye = onehot(iota((W, W), 0) == iota((W, W), 1))
    for ref, grad in zip((dq_ref, dk_ref, dv_ref), unpack(home, 3, 32, own, fold)):
        ref[...] = mm_nt(eye, grad).astype(BF)
    proj_ref[...] = proj_in[0:9, 0:W] * GRAD_SCALE
    total = h_in[0] + h_in[1] + h_in[2] + h_in[3]
    for j in range(3):
        gate_ref[:, 384 * j : 384 * j + 384] = total[1 + j : 2 + j] * GRAD_SCALE


def body(queries, key_heads, value_heads, out_grad, out_proj, gate_scale):
    hbm = pl.BlockSpec(memory_space=pltpu.HBM)
    vmem = pl.BlockSpec(memory_space=pltpu.VMEM)
    token = pltpu.VMEM((W, N), BF)
    home, proj, gate = pl.pallas_call(
        kernel,
        out_shape=(
            jax.ShapeDtypeStruct((32, 32, N), BF),
            jax.ShapeDtypeStruct((16, 384), F32),
            jax.ShapeDtypeStruct((4, 8, 384), F32),
        ),
        in_specs=[hbm] * 6,
        out_specs=(hbm,) * 3,
        scratch_shapes=[
            token, token, token, token,
            pltpu.VMEM((W, 1152), BF),
            pltpu.VMEM((1, 1152), F32),
            pltpu.VMEM((32, 16, N), BF),
            pltpu.VMEM((32, 16, N), BF),
            pltpu.VMEM((32, 32, N), BF),
            pltpu.VMEM((32, 32, N), BF),
            pltpu.VMEM((32, 32, N), BF),
            pltpu.VMEM((4, W, N), BF),
            pltpu.VMEM((2, 256, 1152), BF),
            pltpu.VMEM((256, 1152), BF),
            pltpu.VMEM((16, 16, 1152), BF),
            pltpu.VMEM((16, 16, 1152), BF),
            pltpu.VMEM((4, 16, 384), BF),
            pltpu.VMEM((4, 16, 384), BF),
            pltpu.VMEM((16, 384), F32),
            pltpu.SemaphoreType.DMA((8,)),
            pltpu.SemaphoreType.DMA((15,)),
            pltpu.SemaphoreType.DMA((15,)),
        ],
        compiler_params=pltpu.CompilerParams(
            collective_id=0, has_side_effects=True, vmem_limit_bytes=60 * 1024 * 1024
        ),
    )(queries.T, key_heads.T, value_heads.T, out_grad.T, out_proj.T, gate_scale)
    dq, dk, dv, proj, gate = pl.pallas_call(
        finish,
        out_shape=(
            jax.ShapeDtypeStruct((W, N), BF),
            jax.ShapeDtypeStruct((W, N), BF),
            jax.ShapeDtypeStruct((W, N), BF),
            jax.ShapeDtypeStruct((9, W), F32),
            jax.ShapeDtypeStruct((1, 1152), F32),
        ),
        in_specs=[vmem] * 3,
        out_specs=(vmem,) * 5,
        compiler_params=pltpu.CompilerParams(vmem_limit_bytes=60 * 1024 * 1024),
    )(home, proj, gate)
    return dq.T, dk.T, dv.T, proj, gate


def solution(mesh):
    placed = (
        P("seq", "head"),
        P("seq", "head"),
        P("seq", "head"),
        P("seq", "head"),
        P(None, "head"),
        P(),
    )
    return jax.shard_map(
        body,
        mesh=mesh,
        in_specs=placed,
        out_specs=(P("seq", "head"), P("seq", "head"), P("seq", "head"), P("seq", "head"), P()),
        check_vma=False,
    )
```

```python
import math

import jax
import jax.numpy as jnp
from jax import lax
from jax.experimental import pallas as pl
from jax.experimental.pallas import tpu as pltpu
from jax.sharding import PartitionSpec as P

MESH = pl.DeviceIdType.MESH
BF = jnp.bfloat16
F32 = jnp.float32
HEAD_DIM = 72
TF = 32
P_SIZE = 512
W = 288
N = 128
SCALE = HEAD_DIM ** (-0.5)
GRAD_SCALE = 1.0 / math.sqrt(TF * P_SIZE)


def iota(shape, dim):
    return lax.broadcasted_iota(jnp.int32, shape, dim)


def onehot(cond):
    return jnp.where(cond, 1.0, 0.0).astype(BF)


def mm(a, b):
    return jnp.dot(a, b, preferred_element_type=F32)


def mm_nt(a, b):
    return lax.dot_general(a, b, (((1,), (1,)), ((), ())), preferred_element_type=F32)


def mm_tn(a, b):
    return lax.dot_general(a, b, (((0,), (0,)), ((), ())), preferred_element_type=F32)


def masks():
    own = onehot(iota((N, N), 1) // 32 == iota((N, N), 0) % 4)
    fold = onehot(iota((N, 32), 0) % 32 == iota((N, 32), 1))
    return own, fold


def target(c, n, rows):
    b, j, p = c // 32, (c % 32) // 4, c % 4
    return j * rows + jnp.where(b < 2 * n, 4 * b + p, 6 * n + b)


def pack(arrays, rows, own, fold, dst):
    n = len(arrays)
    sel = onehot(iota((8 * rows, 288 * n // 3), 0) == target(iota((1, 288 * n // 3), 1), n, rows))
    tails = [lax.dot_general(x[:, 256:W], fold, (((1,), (1,)), ((), ())), preferred_element_type=F32).astype(BF) * own for x in arrays]
    for g in range(4):
        at = slice(32 * g, 32 * g + 32)
        stack = [x[at, N * t : N * t + N] for x in arrays for t in range(2)] + [x[at] for x in tails]
        dst[8 * g : 8 * g + 8] = mm(sel, jnp.concatenate(stack, axis=0)).astype(BF).reshape(8, rows, N)


def unpack(src, n, rows, own, fold):
    sel = onehot(iota((288 * n // 3, 8 * rows), 1) == target(iota((288 * n // 3, 1), 0), n, rows))
    parts = [mm(sel, src[8 * g : 8 * g + 8].reshape(8 * rows, N)).astype(BF) for g in range(4)]

    def tile(b):
        return jnp.concatenate([p[32 * b : 32 * b + 32] for p in parts], axis=0)

    return [
        jnp.concatenate([tile(2 * a), tile(2 * a + 1), mm(tile(2 * n + a) * own, fold).astype(BF)], axis=1)
        for a in range(n)
    ]


def kernel(
    q_hbm, k_hbm, v_hbm, g_hbm, w_hbm, s_hbm,
    home, proj_out, gates,
    q_in, k_in, v_in, g_in, w_in, s_in,
    g_send, g_recv, send, recv, back,
    w4, s4, og_all, rs_a, rs_b, c_a, c_b, plane_a, plane_b, got_a, got_b,
    z_send, z_recv, z_sum, gate_send,
    in_sem, s_sem, r_sem,
):
    i = lax.axis_index("seq")
    h = lax.axis_index("head")
    f = i // 4
    r = i % 4
    core = i % 2
    y = (i // 2) % 4
    x = (i // 8) % 4
    z = i // 32
    xy = x * 4 + y

    loads = []
    for n, (src, dst) in enumerate(
        ((g_hbm, g_in), (q_hbm, q_in), (k_hbm, k_in), (v_hbm, v_in), (w_hbm, w_in), (s_hbm, s_in))
    ):
        copy = pltpu.make_async_copy(src, dst, in_sem.at[n])
        copy.start()
        loads.append(copy)

    barrier = pltpu.get_barrier_semaphore()

    def greet(seq, head):
        pl.semaphore_signal(barrier, inc=1, device_id=(seq, head), device_id_type=MESH)

    greet(i, (h + 1) % 4)
    greet(i, (h + 3) % 4)

    def greet_frames(t, carry):
        greet(4 * ((f + t) % 32) + r, h)
        return carry

    lax.fori_loop(1, 32, greet_frames, 0)

    def greet_plane(t, carry):
        greet(((z * 4 + t // 2) * 4 + 2 * (t % 2) + 1 - y % 2) * 2 + core, h)
        return carry

    lax.fori_loop(0, 8, greet_plane, 0)
    greet(i + 1 - 2 * core, h)

    own, fold = masks()
    eye = onehot(iota((N, N), 0) == iota((N, N), 1))

    def scatter(src, dst, n):
        pltpu.make_async_copy(src.at[f], dst.at[f], r_sem.at[n]).start()

        def one(t, carry):
            j = (f + t) % 32
            pltpu.make_async_remote_copy(
                src.at[j], dst.at[f], s_sem.at[n], r_sem.at[n],
                device_id=(4 * j + r, h), device_id_type=MESH,
            ).start()
            return carry

        lax.fori_loop(1, 32, one, 0)

    def wait_all(ref, sem):
        pltpu.make_async_copy(ref, ref, sem).wait()

    loads[0].wait()
    pack([mm_nt(eye, g_in[...]).astype(BF)], 16, own, fold, g_send)
    pl.semaphore_wait(barrier, 42)
    scatter(g_send, g_recv, 14)
    for copy in loads[1:4]:
        copy.wait()
    pack([mm_nt(eye, ref[...]).astype(BF) for ref in (q_in, k_in, v_in)], 32, own, fold, send)
    scatter(send, recv, 0)

    heads = [onehot(iota((1, W), 1) // HEAD_DIM == k) for k in range(4)]
    same = iota((N, N), 0) % 4 == iota((N, N), 1) % 4
    drow, dcol = iota((512, W), 0), iota((512, W), 1)
    blk, kk = drow // 16, drow % 16
    spread = onehot(jnp.logical_and(kk < 9, dcol == (blk % 16) * 18 + blk // 16 * 9 + kk))
    crow, ccol = iota((72, N), 0), iota((72, N), 1)
    squeeze = onehot(
        ccol == jnp.where(crow < 64, (crow % 32) // 4 * 16 + crow // 32 * 4 + crow % 4, (crow - 64) * 16 + 8)
    )
    repeat = onehot(iota((N, 32), 0) // 4 == iota((N, 32), 1))
    prow, pcol = iota((W, N), 0), iota((W, N), 1)
    place = [onehot(jnp.logical_and(pcol // 32 == k, prow == 256 + pcol - 32 * k)) for k in range(4)]
    is_gate = iota((512, 1), 0) % 16 == 9

    wait_all(g_recv, r_sem.at[14])
    parts = [mm(squeeze, g_recv[8 * g : 8 * g + 8].reshape(N, N)).astype(BF) for g in range(4)]
    og_all[h] = jnp.concatenate(
        [p[0:32] for p in parts] + [p[32:64] for p in parts]
        + [jnp.concatenate([p[64:72] for p in parts], axis=0)],
        axis=0,
    )

    right, left = (h + 1) % 4, (h + 3) % 4
    first, second = pl.ds(0, 144), pl.ds(144, 144)

    def pass_on(slot, rows, peer, n):
        return pltpu.make_async_remote_copy(
            og_all.at[slot, rows], og_all.at[slot, rows], s_sem.at[n], r_sem.at[n],
            device_id=(i, peer), device_id_type=MESH,
        )

    ring = [
        pass_on(h, first, right, 5), pass_on(h, second, left, 6),
        pass_on(h, second, right, 7), pass_on(h, first, left, 8),
    ]
    for copy in ring:
        copy.start()

    loads[4].wait()
    loads[5].wait()
    for n in range(4):
        w4[n] = w_in[:, W * n : W * n + W]
        s4[n] = s_in[:, W * n : W * n + W]

    ring[0].wait_recv()
    far = [pass_on(left, first, right, 9)]
    far[0].start()
    ring[1].wait_recv()
    far.append(pass_on(right, second, left, 10))
    far[1].start()

    wait_all(recv, r_sem.at[0])
    q, k, v = unpack(recv, 3, 32, own, fold)
    km = jnp.concatenate([k * m for m in heads], axis=0)
    vm = jnp.concatenate([v * m for m in heads], axis=0)
    scores = mm_nt(q, km) * SCALE
    probs = []
    for n in range(4):
        sc = jnp.where(same, scores[:, N * n : N * n + N], -1e30)
        e = jnp.where(same, jnp.exp(sc - jnp.max(sc, axis=-1, keepdims=True)), 0.0)
        probs.append(e / jnp.sum(e, axis=-1, keepdims=True))
    light = [p.astype(BF) for p in probs]
    out = mm(jnp.concatenate(light, axis=1), vm).astype(BF)

    def shard(n, role):
        tail = mm(mm(repeat, og_all[n, 256:288]).astype(BF) * own, fold)
        up = jnp.concatenate([og_all[n, 0:128].astype(F32), og_all[n, 128:256].astype(F32), tail], axis=1)
        scaled = (up * s4[n]).astype(BF)
        wn = w4[n]
        gate_row = jnp.sum(up * mm(out, wn), axis=0, keepdims=True)
        scaled_t = mm_nt(spread, scaled).astype(BF)
        main = jnp.where(is_gate, gate_row[:, :256], mm(scaled_t, out[:, :256])).astype(BF)
        gate_tail = mm(gate_row.astype(BF), place[role])
        tail = jnp.where(is_gate, gate_tail, mm(scaled_t, mm(out, place[role]).astype(BF)))
        return mm_nt(scaled, wn), main, tail

    def halves(a):
        return a.reshape(2, 256, N)

    sibling = (i + 1 - 2 * core, h)

    def to_sibling(src, dst, n):
        copy = pltpu.make_async_remote_copy(
            src.at[:, 1 - core], dst, s_sem.at[n], r_sem.at[n], device_id=sibling, device_id_type=MESH
        )
        copy.start()
        return copy

    def to_plane(src, dst, n):
        pltpu.make_async_copy(src.at[:, xy], dst.at[xy], r_sem.at[n]).start()

        def one(t, carry):
            j = (xy + t) % 16
            pltpu.make_async_remote_copy(
                src.at[:, j], dst.at[xy], s_sem.at[n], r_sem.at[n],
                device_id=((z * 16 + j) * 2 + core, h), device_id_type=MESH,
            ).start()
            return carry

        lax.fori_loop(1, 16, one, 0)

    do, main, tail_acc = shard(h, 0)
    rs_a[0], rs_a[1] = halves(main[:, :128]), halves(main[:, 128:])
    ring[2].wait_recv()
    ring[3].wait_recv()
    for role, n in ((1, left), (2, right)):
        term, main, tail = shard(n, role)
        do += term
        tail_acc += tail
        rs_a[2 * role], rs_a[2 * role + 1] = halves(main[:, :128]), halves(main[:, 128:])
    rs_a[6] = halves(tail_acc.astype(BF))
    pair_a = to_sibling(rs_a, c_a, 1)
    pair_a.wait()
    plane_a[...] = (
        (rs_a[:, core].astype(F32) + c_a[...].astype(F32)).astype(BF).reshape(7, 16, 16, N)
    )
    to_plane(plane_a, got_a, 3)

    for copy in far:
        copy.wait_recv()
    term, main, tail = shard((h + 2) % 4, 3)
    rs_b[0], rs_b[1], rs_b[2] = halves(main[:, :128]), halves(main[:, 128:]), halves(tail.astype(BF))
    pair_b = to_sibling(rs_b, c_b, 15)

    do = (do + term).astype(BF)
    dprob = mm_nt(do, vm)
    dlight = []
    for n in range(4):
        dp = dprob[:, N * n : N * n + N]
        delta = jnp.sum(light[n].astype(F32) * dp, axis=-1, keepdims=True)
        dlight.append((probs[n] * (dp - delta)).astype(BF))

    pair_b.wait()
    plane_b[...] = (
        (rs_b[:, core].astype(F32) + c_b[...].astype(F32)).astype(BF).reshape(3, 16, 16, N)
    )
    to_plane(plane_b, got_b, 16)

    dq = (mm(jnp.concatenate(dlight, axis=1), km) * SCALE).astype(BF)
    qm = jnp.concatenate([q * m for m in heads], axis=0)
    dom = jnp.concatenate([do * m for m in heads], axis=0)
    dk = (mm_tn(jnp.concatenate(dlight, axis=0), qm) * SCALE).astype(BF)
    dv = mm_tn(jnp.concatenate(light, axis=0), dom).astype(BF)
    pack([dq, dk, dv], 32, own, fold, back)
    scatter(back, home, 2)

    wait_all(got_a, r_sem.at[3])
    sum_a = got_a[0].astype(F32)
    for n in range(1, 16):
        sum_a += got_a[n].astype(F32)
    wait_all(got_b, r_sem.at[16])
    sum_b = got_b[0].astype(F32)
    for n in range(1, 16):
        sum_b += got_b[n].astype(F32)
    tail = sum_a[6] + sum_b[2]
    tiles = [sum_a[n] for n in range(6)] + [sum_b[0], sum_b[1], tail]

    gate_send[...] = jnp.concatenate([t[9:10] for t in tiles] + [jnp.zeros((7, N), F32)], axis=0).astype(BF)
    slot = h * 4 + z
    pltpu.make_async_copy(gate_send, gates.at[slot], r_sem.at[11]).start()

    def to_line(t, carry):
        j = (slot + t) % 16
        pltpu.make_async_remote_copy(
            gate_send, gates.at[slot], s_sem.at[11], r_sem.at[11],
            device_id=(j % 4 * 32 + i % 32, j // 4), device_id_type=MESH,
        ).start()
        return carry

    lax.fori_loop(1, 16, to_line, 0)

    tail = tail.astype(BF)
    for role, n in ((0, h), (1, left), (2, right), (3, (h + 2) % 4)):
        back_to_0 = onehot(jnp.logical_and(iota((N, N), 0) == 32 * role + iota((N, N), 1), iota((N, N), 1) < 32))
        z_send[n] = jnp.concatenate(
            [tiles[2 * role].astype(BF), tiles[2 * role + 1].astype(BF), mm(tail, back_to_0).astype(BF)], axis=1
        )
    pltpu.make_async_copy(z_send.at[z], z_recv.at[z], r_sem.at[4]).start()
    for t in range(1, 4):
        j = (z + t) % 4
        pltpu.make_async_remote_copy(
            z_send.at[j], z_recv.at[z], s_sem.at[4], r_sem.at[4],
            device_id=(j * 32 + i % 32, h), device_id_type=MESH,
        ).start()
    wait_all(z_recv, r_sem.at[4])
    total = z_recv[0].astype(F32)
    for n in range(1, 4):
        total += z_recv[n].astype(F32)
    z_sum[...] = total
    store = pltpu.make_async_copy(z_sum, proj_out, in_sem.at[6])
    store.start()

    for copy in ring + far:
        copy.wait_send()
    wait_all(g_send.at[pl.ds(0, 31)], s_sem.at[14])
    wait_all(send.at[pl.ds(0, 31)], s_sem.at[0])
    wait_all(back.at[pl.ds(0, 31)], s_sem.at[2])
    wait_all(plane_a.at[:, pl.ds(0, 15)], s_sem.at[3])
    wait_all(plane_b.at[:, pl.ds(0, 15)], s_sem.at[16])
    wait_all(z_send.at[pl.ds(0, 3)], s_sem.at[4])
    wait_all(gates.at[pl.ds(0, 15)], s_sem.at[11])
    wait_all(home, r_sem.at[2])
    wait_all(gates, r_sem.at[11])
    store.wait()


def finish(home, proj_in, gates, dq_ref, dk_ref, dv_ref, proj_ref, gate_ref):
    own, fold = masks()
    eye = onehot(iota((W, W), 0) == iota((W, W), 1))
    for ref, grad in zip((dq_ref, dk_ref, dv_ref), unpack(home, 3, 32, own, fold)):
        ref[...] = mm_nt(eye, grad).astype(BF)
    proj_ref[...] = proj_in[0:9, 0:W] * GRAD_SCALE
    rows = [[] for n in range(4)]
    for h in range(4):
        total = gates[4 * h].astype(F32)
        for z in range(1, 4):
            total += gates[4 * h + z].astype(F32)
        for role, n in enumerate((h, (h + 3) % 4, (h + 1) % 4, (h + 2) % 4)):
            rows[n].append(jnp.concatenate(
                [total[2 * role : 2 * role + 1], total[2 * role + 1 : 2 * role + 2], total[8:9, 32 * role : 32 * role + 32]], axis=1
            ))
    gate_ref[...] = jnp.concatenate([a + b + c + d for a, b, c, d in rows], axis=1) * GRAD_SCALE


def body(queries, key_heads, value_heads, out_grad, out_proj, gate_scale):
    hbm = pl.BlockSpec(memory_space=pltpu.HBM)
    vmem = pl.BlockSpec(memory_space=pltpu.VMEM)
    token = pltpu.VMEM((W, N), BF)
    home, proj, gate = pl.pallas_call(
        kernel,
        out_shape=(
            jax.ShapeDtypeStruct((32, 32, N), BF),
            jax.ShapeDtypeStruct((16, 384), F32),
            jax.ShapeDtypeStruct((16, 16, N), BF),
        ),
        in_specs=[hbm] * 6,
        out_specs=(hbm,) * 3,
        scratch_shapes=[
            token, token, token, token,
            pltpu.VMEM((W, 1152), BF),
            pltpu.VMEM((1, 1152), F32),
            pltpu.VMEM((32, 16, N), BF),
            pltpu.VMEM((32, 16, N), BF),
            pltpu.VMEM((32, 32, N), BF),
            pltpu.VMEM((32, 32, N), BF),
            pltpu.VMEM((32, 32, N), BF),
            pltpu.VMEM((4, W, W), BF),
            pltpu.VMEM((4, 1, W), F32),
            pltpu.VMEM((4, W, N), BF),
            pltpu.VMEM((7, 2, 256, N), BF),
            pltpu.VMEM((3, 2, 256, N), BF),
            pltpu.VMEM((7, 256, N), BF),
            pltpu.VMEM((3, 256, N), BF),
            pltpu.VMEM((7, 16, 16, N), BF),
            pltpu.VMEM((3, 16, 16, N), BF),
            pltpu.VMEM((16, 7, 16, N), BF),
            pltpu.VMEM((16, 3, 16, N), BF),
            pltpu.VMEM((4, 16, 384), BF),
            pltpu.VMEM((4, 16, 384), BF),
            pltpu.VMEM((16, 384), F32),
            pltpu.VMEM((16, N), BF),
            pltpu.SemaphoreType.DMA((8,)),
            pltpu.SemaphoreType.DMA((17,)),
            pltpu.SemaphoreType.DMA((17,)),
        ],
        compiler_params=pltpu.CompilerParams(
            collective_id=0, has_side_effects=True, vmem_limit_bytes=60 * 1024 * 1024
        ),
    )(queries.T, key_heads.T, value_heads.T, out_grad.T, out_proj.T, gate_scale)
    dq, dk, dv, proj, gate = pl.pallas_call(
        finish,
        out_shape=(
            jax.ShapeDtypeStruct((W, N), BF),
            jax.ShapeDtypeStruct((W, N), BF),
            jax.ShapeDtypeStruct((W, N), BF),
            jax.ShapeDtypeStruct((9, W), F32),
            jax.ShapeDtypeStruct((1, 1152), F32),
        ),
        in_specs=[vmem] * 3,
        out_specs=(vmem,) * 5,
        compiler_params=pltpu.CompilerParams(vmem_limit_bytes=60 * 1024 * 1024),
    )(home, proj, gate)
    return dq.T, dk.T, dv.T, proj, gate


def solution(mesh):
    placed = (
        P("seq", "head"),
        P("seq", "head"),
        P("seq", "head"),
        P("seq", "head"),
        P(None, "head"),
        P(),
    )
    return jax.shard_map(
        body,
        mesh=mesh,
        in_specs=placed,
        out_specs=(P("seq", "head"), P("seq", "head"), P("seq", "head"), P("seq", "head"), P()),
        check_vma=False,
    )
```

```python
import math

import jax
import jax.numpy as jnp
from jax import lax
from jax.experimental import pallas as pl
from jax.experimental.pallas import tpu as pltpu
from jax.sharding import PartitionSpec as P

MESH = pl.DeviceIdType.MESH
BF = jnp.bfloat16
F32 = jnp.float32
HEAD_DIM = 72
TF = 32
P_SIZE = 512
W = 288
N = 128
SCALE = HEAD_DIM ** (-0.5)
GRAD_SCALE = 1.0 / math.sqrt(TF * P_SIZE)


def iota(shape, dim):
    return lax.broadcasted_iota(jnp.int32, shape, dim)


def onehot(cond):
    return jnp.where(cond, 1.0, 0.0).astype(BF)


def mm(a, b):
    return jnp.dot(a, b, preferred_element_type=F32)


def mm_nt(a, b):
    return lax.dot_general(a, b, (((1,), (1,)), ((), ())), preferred_element_type=F32)


def mm_tn(a, b):
    return lax.dot_general(a, b, (((0,), (0,)), ((), ())), preferred_element_type=F32)


def masks():
    own = onehot(iota((N, N), 1) // 32 == iota((N, N), 0) % 4)
    fold = onehot(iota((N, 32), 0) % 32 == iota((N, 32), 1))
    return own, fold


def target(c, n, rows):
    b, j, p = c // 32, (c % 32) // 4, c % 4
    return j * rows + jnp.where(b < 2 * n, 4 * b + p, 6 * n + b)


def pack(arrays, rows, own, fold, dst):
    n = len(arrays)
    sel = onehot(iota((8 * rows, 288 * n // 3), 0) == target(iota((1, 288 * n // 3), 1), n, rows))
    tails = [lax.dot_general(x[:, 256:W], fold, (((1,), (1,)), ((), ())), preferred_element_type=F32).astype(BF) * own for x in arrays]
    for g in range(4):
        at = slice(32 * g, 32 * g + 32)
        stack = [x[at, N * t : N * t + N] for x in arrays for t in range(2)] + [x[at] for x in tails]
        dst[8 * g : 8 * g + 8] = mm(sel, jnp.concatenate(stack, axis=0)).astype(BF).reshape(8, rows, N)


def unpack(src, n, rows, own, fold):
    sel = onehot(iota((288 * n // 3, 8 * rows), 1) == target(iota((288 * n // 3, 1), 0), n, rows))
    parts = [mm(sel, src[8 * g : 8 * g + 8].reshape(8 * rows, N)).astype(BF) for g in range(4)]

    def tile(b):
        return jnp.concatenate([p[32 * b : 32 * b + 32] for p in parts], axis=0)

    return [
        jnp.concatenate([tile(2 * a), tile(2 * a + 1), mm(tile(2 * n + a) * own, fold).astype(BF)], axis=1)
        for a in range(n)
    ]


def kernel(
    q_hbm, k_hbm, v_hbm, g_hbm, w_hbm, s_hbm,
    home, proj_out, gates,
    q_in, k_in, v_in, g_in, w_in, s_in,
    g_send, g_recv, send, recv, back,
    w4, s4, og_all, rs_o, rs_a, rs_b, c_o, c_a, c_b, plane_o, plane_a, plane_b, got_o, got_a, got_b,
    z_send, z_recv, z_sum, gate_send,
    in_sem, s_sem, r_sem, ag_sem, ready,
):
    i = lax.axis_index("seq")
    h = lax.axis_index("head")
    f = i // 4
    r = i % 4
    core = i % 2
    y = (i // 2) % 4
    x = (i // 8) % 4
    z = i // 32
    xy = x * 4 + y

    loads = []
    for n, (src, dst) in enumerate(
        ((g_hbm, g_in), (q_hbm, q_in), (k_hbm, k_in), (v_hbm, v_in), (w_hbm, w_in), (s_hbm, s_in))
    ):
        copy = pltpu.make_async_copy(src, dst, in_sem.at[n])
        copy.start()
        loads.append(copy)

    barrier = pltpu.get_barrier_semaphore()

    def greet(seq, head):
        pl.semaphore_signal(barrier, inc=1, device_id=(seq, head), device_id_type=MESH)

    odd = h % 2
    near = 1 - odd
    late = 3 - odd

    @pl.when(h == 0)
    def _():
        greet(i, 1)
        greet(i, 3)

    @pl.when(odd == 1)
    def _():
        greet(i, 2)


    def greet_frames(t, carry):
        greet(4 * ((f + t) % 32) + r, h)
        return carry

    lax.fori_loop(1, 32, greet_frames, 0)

    def greet_plane(t, carry):
        greet(((z * 4 + t // 2) * 4 + 2 * (t % 2) + 1 - y % 2) * 2 + core, h)
        return carry

    lax.fori_loop(0, 8, greet_plane, 0)
    greet(i + 1 - 2 * core, h)

    own, fold = masks()
    eye = onehot(iota((N, N), 0) == iota((N, N), 1))

    def scatter(src, dst, n):
        pltpu.make_async_copy(src.at[f], dst.at[f], r_sem.at[n]).start()

        def one(t, carry):
            j = (f + t) % 32
            pltpu.make_async_remote_copy(
                src.at[j], dst.at[f], s_sem.at[n], r_sem.at[n],
                device_id=(4 * j + r, h), device_id_type=MESH,
            ).start()
            return carry

        lax.fori_loop(1, 32, one, 0)

    def wait_all(ref, sem):
        pltpu.make_async_copy(ref, ref, sem).wait()

    loads[0].wait()
    pack([mm_nt(eye, g_in[...]).astype(BF)], 16, own, fold, g_send)
    pl.semaphore_wait(barrier, 40 + jnp.minimum(h, 4 - h))

    @pl.when(odd == 1)
    def _():
        pl.semaphore_signal(ready, inc=1, device_id=(i, 0), device_id_type=MESH)

    @pl.when(h == 2)
    def _():
        pl.semaphore_signal(ready, inc=1, device_id=(i, 1), device_id_type=MESH)
        pl.semaphore_signal(ready, inc=1, device_id=(i, 3), device_id_type=MESH)

    scatter(g_send, g_recv, 14)
    for copy in loads[1:4]:
        copy.wait()
    pack([mm_nt(eye, ref[...]).astype(BF) for ref in (q_in, k_in, v_in)], 32, own, fold, send)
    scatter(send, recv, 0)

    heads = [onehot(iota((1, W), 1) // HEAD_DIM == k) for k in range(4)]
    same = iota((N, N), 0) % 4 == iota((N, N), 1) % 4
    drow, dcol = iota((512, W), 0), iota((512, W), 1)
    blk, kk = drow // 16, drow % 16
    spread = onehot(jnp.logical_and(kk < 9, dcol == (blk % 16) * 18 + blk // 16 * 9 + kk))
    crow, ccol = iota((72, N), 0), iota((72, N), 1)
    squeeze = onehot(
        ccol == jnp.where(crow < 64, (crow % 32) // 4 * 16 + crow // 32 * 4 + crow % 4, (crow - 64) * 16 + 8)
    )
    repeat = onehot(iota((N, 32), 0) // 4 == iota((N, 32), 1))
    prow, pcol = iota((W, N), 0), iota((W, N), 1)
    place = [onehot(jnp.logical_and(pcol // 32 == k, prow == 256 + pcol - 32 * k)) for k in range(4)]
    is_gate = iota((512, 1), 0) % 16 == 9

    wait_all(g_recv, r_sem.at[14])
    parts = [mm(squeeze, g_recv[8 * g : 8 * g + 8].reshape(N, N)).astype(BF) for g in range(4)]
    og_all[h] = jnp.concatenate(
        [p[0:32] for p in parts] + [p[32:64] for p in parts]
        + [jnp.concatenate([p[64:72] for p in parts], axis=0)],
        axis=0,
    )

    near_half = jnp.where(near == (h + 1) % 4, 1, 0)
    late_half = 1 - near_half

    def pass_on(slot, half, peer, n):
        rows = pl.ds(pl.multiple_of(half * 144, 16), 144)
        copy = pltpu.make_async_remote_copy(
            og_all.at[slot, rows], og_all.at[slot, rows], s_sem.at[n], ag_sem.at[slot, half],
            device_id=(i, peer), device_id_type=MESH,
        )
        copy.start()
        return copy

    def arrived(slot, half):
        rows = pl.ds(pl.multiple_of(half * 144, 16), 144)
        wait_all(og_all.at[slot, rows], ag_sem.at[slot, half])

    @pl.when(h == 0)
    def _():
        pl.semaphore_wait(ready, 2)

    ring = [pass_on(h, late_half, near, 5), pass_on(h, near_half, near, 6)]

    @pl.when(odd == 1)
    def _():
        pl.semaphore_wait(ready, 1)

    ring += [pass_on(h, near_half, late, 7), pass_on(h, late_half, late, 8)]

    loads[4].wait()
    loads[5].wait()
    for n in range(4):
        w4[n] = w_in[:, W * n : W * n + W]
        s4[n] = s_in[:, W * n : W * n + W]

    arrived(near, near_half)
    ring.append(pass_on(near, near_half, late, 9))

    wait_all(recv, r_sem.at[0])
    q, k, v = unpack(recv, 3, 32, own, fold)
    km = jnp.concatenate([k * m for m in heads], axis=0)
    vm = jnp.concatenate([v * m for m in heads], axis=0)
    scores = mm_nt(q, km) * SCALE
    probs = []
    for n in range(4):
        sc = jnp.where(same, scores[:, N * n : N * n + N], -1e30)
        e = jnp.where(same, jnp.exp(sc - jnp.max(sc, axis=-1, keepdims=True)), 0.0)
        probs.append(e / jnp.sum(e, axis=-1, keepdims=True))
    light = [p.astype(BF) for p in probs]
    out = mm(jnp.concatenate(light, axis=1), vm).astype(BF)

    def shard(n, role):
        tail = mm(mm(repeat, og_all[n, 256:288]).astype(BF) * own, fold)
        up = jnp.concatenate([og_all[n, 0:128].astype(F32), og_all[n, 128:256].astype(F32), tail], axis=1)
        scaled = (up * s4[n]).astype(BF)
        wn = w4[n]
        gate_row = jnp.sum(up * mm(out, wn), axis=0, keepdims=True)
        scaled_t = mm_nt(spread, scaled).astype(BF)
        main = jnp.where(is_gate, gate_row[:, :256], mm(scaled_t, out[:, :256])).astype(BF)
        gate_tail = mm(gate_row.astype(BF), place[role])
        tail = jnp.where(is_gate, gate_tail, mm(scaled_t, mm(out, place[role]).astype(BF)))
        return mm_nt(scaled, wn), main, tail

    def halves(a):
        return a.reshape(2, 256, N)

    sibling = (i + 1 - 2 * core, h)

    def to_sibling(src, dst, n):
        copy = pltpu.make_async_remote_copy(
            src.at[:, 1 - core], dst, s_sem.at[n], r_sem.at[n], device_id=sibling, device_id_type=MESH
        )
        copy.start()
        return copy

    def to_plane(src, dst, n):
        pltpu.make_async_copy(src.at[:, xy], dst.at[xy], r_sem.at[n]).start()

        def one(t, carry):
            j = (xy + t) % 16
            pltpu.make_async_remote_copy(
                src.at[:, j], dst.at[xy], s_sem.at[n], r_sem.at[n],
                device_id=((z * 16 + j) * 2 + core, h), device_id_type=MESH,
            ).start()
            return carry

        lax.fori_loop(1, 16, one, 0)

    def summed(rs, got, n):
        return (rs[:, core].astype(F32) + got[...].astype(F32)).astype(BF).reshape(n, 16, 16, N)

    do, main, tail_acc = shard(h, 0)
    rs_o[0], rs_o[1] = halves(main[:, :128]), halves(main[:, 128:])
    pair_o = to_sibling(rs_o, c_o, 1)
    arrived(late, late_half)
    ring.append(pass_on(late, late_half, near, 10))
    pair_o.wait()
    plane_o[...] = summed(rs_o, c_o, 2)
    to_plane(plane_o, got_o, 12)

    last = jnp.where(h == 2, 0, 2)
    others = (1 - odd, jnp.where(h == 3, 1, 3), last)

    def await_shard(n):
        for half in range(2):
            seen = jnp.logical_or(
                jnp.logical_and(n == near, near_half == half), jnp.logical_and(n == late, late_half == half)
            )

            @pl.when(jnp.logical_not(seen))
            def _():
                arrived(n, half)

    for role in (1, 2):
        await_shard(others[role - 1])
        term, main, tail = shard(others[role - 1], role)
        do += term
        tail_acc += tail
        rs_a[2 * role - 2], rs_a[2 * role - 1] = halves(main[:, :128]), halves(main[:, 128:])
    rs_a[4] = halves(tail_acc.astype(BF))
    pair_a = to_sibling(rs_a, c_a, 13)
    pair_a.wait()
    plane_a[...] = summed(rs_a, c_a, 5)
    to_plane(plane_a, got_a, 3)

    await_shard(last)
    term, main, tail = shard(last, 3)
    rs_b[0], rs_b[1], rs_b[2] = halves(main[:, :128]), halves(main[:, 128:]), halves(tail.astype(BF))
    pair_b = to_sibling(rs_b, c_b, 15)

    do = (do + term).astype(BF)
    dprob = mm_nt(do, vm)
    dlight = []
    for n in range(4):
        dp = dprob[:, N * n : N * n + N]
        delta = jnp.sum(light[n].astype(F32) * dp, axis=-1, keepdims=True)
        dlight.append((probs[n] * (dp - delta)).astype(BF))

    pair_b.wait()
    plane_b[...] = summed(rs_b, c_b, 3)
    to_plane(plane_b, got_b, 16)

    dq = (mm(jnp.concatenate(dlight, axis=1), km) * SCALE).astype(BF)
    qm = jnp.concatenate([q * m for m in heads], axis=0)
    dom = jnp.concatenate([do * m for m in heads], axis=0)
    dk = (mm_tn(jnp.concatenate(dlight, axis=0), qm) * SCALE).astype(BF)
    dv = mm_tn(jnp.concatenate(light, axis=0), dom).astype(BF)
    pack([dq, dk, dv], 32, own, fold, back)
    scatter(back, home, 2)

    def sum_plane(got, n):
        wait_all(got, r_sem.at[n])
        total = got[0].astype(F32)
        for m in range(1, 16):
            total += got[m].astype(F32)
        return total

    sum_o = sum_plane(got_o, 12)
    sum_a = sum_plane(got_a, 3)
    sum_b = sum_plane(got_b, 16)
    tail = sum_a[4] + sum_b[2]
    tiles = [sum_o[0], sum_o[1]] + [sum_a[n] for n in range(4)] + [sum_b[0], sum_b[1], tail]

    gate_send[...] = jnp.concatenate([t[9:10] for t in tiles] + [jnp.zeros((7, N), F32)], axis=0).astype(BF)
    slot = h * 4 + z
    pltpu.make_async_copy(gate_send, gates.at[slot], r_sem.at[11]).start()

    def to_line(t, carry):
        j = (slot + t) % 16
        pltpu.make_async_remote_copy(
            gate_send, gates.at[slot], s_sem.at[11], r_sem.at[11],
            device_id=(j % 4 * 32 + i % 32, j // 4), device_id_type=MESH,
        ).start()
        return carry

    lax.fori_loop(1, 16, to_line, 0)

    tail = tail.astype(BF)
    for role, n in enumerate((h,) + others):
        back_to_0 = onehot(jnp.logical_and(iota((N, N), 0) == 32 * role + iota((N, N), 1), iota((N, N), 1) < 32))
        z_send[n] = jnp.concatenate(
            [tiles[2 * role].astype(BF), tiles[2 * role + 1].astype(BF), mm(tail, back_to_0).astype(BF)], axis=1
        )
    pltpu.make_async_copy(z_send.at[z], z_recv.at[z], r_sem.at[4]).start()
    for t in range(1, 4):
        j = (z + t) % 4
        pltpu.make_async_remote_copy(
            z_send.at[j], z_recv.at[z], s_sem.at[4], r_sem.at[4],
            device_id=(j * 32 + i % 32, h), device_id_type=MESH,
        ).start()
    wait_all(z_recv, r_sem.at[4])
    total = z_recv[0].astype(F32)
    for n in range(1, 4):
        total += z_recv[n].astype(F32)
    z_sum[...] = total
    store = pltpu.make_async_copy(z_sum, proj_out, in_sem.at[6])
    store.start()

    for copy in ring:
        copy.wait_send()
    wait_all(g_send.at[pl.ds(0, 31)], s_sem.at[14])
    wait_all(send.at[pl.ds(0, 31)], s_sem.at[0])
    wait_all(back.at[pl.ds(0, 31)], s_sem.at[2])
    wait_all(plane_o.at[:, pl.ds(0, 15)], s_sem.at[12])
    wait_all(plane_a.at[:, pl.ds(0, 15)], s_sem.at[3])
    wait_all(plane_b.at[:, pl.ds(0, 15)], s_sem.at[16])
    wait_all(z_send.at[pl.ds(0, 3)], s_sem.at[4])
    wait_all(gates.at[pl.ds(0, 15)], s_sem.at[11])
    wait_all(home, r_sem.at[2])
    wait_all(gates, r_sem.at[11])
    store.wait()


def finish(home, proj_in, gates, dq_ref, dk_ref, dv_ref, proj_ref, gate_ref):
    own, fold = masks()
    eye = onehot(iota((W, W), 0) == iota((W, W), 1))
    for ref, grad in zip((dq_ref, dk_ref, dv_ref), unpack(home, 3, 32, own, fold)):
        ref[...] = mm_nt(eye, grad).astype(BF)
    proj_ref[...] = proj_in[0:9, 0:W] * GRAD_SCALE
    rows = [[] for n in range(4)]
    for h in range(4):
        total = gates[4 * h].astype(F32)
        for z in range(1, 4):
            total += gates[4 * h + z].astype(F32)
        for role, n in enumerate(((0, 1, 3, 2), (1, 0, 3, 2), (2, 1, 3, 0), (3, 0, 1, 2))[h]):
            rows[n].append(jnp.concatenate(
                [total[2 * role : 2 * role + 1], total[2 * role + 1 : 2 * role + 2], total[8:9, 32 * role : 32 * role + 32]], axis=1
            ))
    gate_ref[...] = jnp.concatenate([a + b + c + d for a, b, c, d in rows], axis=1) * GRAD_SCALE


def body(queries, key_heads, value_heads, out_grad, out_proj, gate_scale):
    hbm = pl.BlockSpec(memory_space=pltpu.HBM)
    vmem = pl.BlockSpec(memory_space=pltpu.VMEM)
    token = pltpu.VMEM((W, N), BF)
    home, proj, gate = pl.pallas_call(
        kernel,
        out_shape=(
            jax.ShapeDtypeStruct((32, 32, N), BF),
            jax.ShapeDtypeStruct((16, 384), F32),
            jax.ShapeDtypeStruct((16, 16, N), BF),
        ),
        in_specs=[hbm] * 6,
        out_specs=(hbm,) * 3,
        scratch_shapes=[
            token, token, token, token,
            pltpu.VMEM((W, 1152), BF),
            pltpu.VMEM((1, 1152), F32),
            pltpu.VMEM((32, 16, N), BF),
            pltpu.VMEM((32, 16, N), BF),
            pltpu.VMEM((32, 32, N), BF),
            pltpu.VMEM((32, 32, N), BF),
            pltpu.VMEM((32, 32, N), BF),
            pltpu.VMEM((4, W, W), BF),
            pltpu.VMEM((4, 1, W), F32),
            pltpu.VMEM((4, W, N), BF),
            pltpu.VMEM((2, 2, 256, N), BF),
            pltpu.VMEM((5, 2, 256, N), BF),
            pltpu.VMEM((3, 2, 256, N), BF),
            pltpu.VMEM((2, 256, N), BF),
            pltpu.VMEM((5, 256, N), BF),
            pltpu.VMEM((3, 256, N), BF),
            pltpu.VMEM((2, 16, 16, N), BF),
            pltpu.VMEM((5, 16, 16, N), BF),
            pltpu.VMEM((3, 16, 16, N), BF),
            pltpu.VMEM((16, 2, 16, N), BF),
            pltpu.VMEM((16, 5, 16, N), BF),
            pltpu.VMEM((16, 3, 16, N), BF),
            pltpu.VMEM((4, 16, 384), BF),
            pltpu.VMEM((4, 16, 384), BF),
            pltpu.VMEM((16, 384), F32),
            pltpu.VMEM((16, N), BF),
            pltpu.SemaphoreType.DMA((8,)),
            pltpu.SemaphoreType.DMA((17,)),
            pltpu.SemaphoreType.DMA((17,)),
            pltpu.SemaphoreType.DMA((4, 2)),
            pltpu.SemaphoreType.REGULAR,
        ],
        compiler_params=pltpu.CompilerParams(
            collective_id=0, has_side_effects=True, vmem_limit_bytes=60 * 1024 * 1024
        ),
    )(queries.T, key_heads.T, value_heads.T, out_grad.T, out_proj.T, gate_scale)
    dq, dk, dv, proj, gate = pl.pallas_call(
        finish,
        out_shape=(
            jax.ShapeDtypeStruct((W, N), BF),
            jax.ShapeDtypeStruct((W, N), BF),
            jax.ShapeDtypeStruct((W, N), BF),
            jax.ShapeDtypeStruct((9, W), F32),
            jax.ShapeDtypeStruct((1, 1152), F32),
        ),
        in_specs=[vmem] * 3,
        out_specs=(vmem,) * 5,
        compiler_params=pltpu.CompilerParams(vmem_limit_bytes=60 * 1024 * 1024),
    )(home, proj, gate)
    return dq.T, dk.T, dv.T, proj, gate


def solution(mesh):
    placed = (
        P("seq", "head"),
        P("seq", "head"),
        P("seq", "head"),
        P("seq", "head"),
        P(None, "head"),
        P(),
    )
    return jax.shard_map(
        body,
        mesh=mesh,
        in_specs=placed,
        out_specs=(P("seq", "head"), P("seq", "head"), P("seq", "head"), P("seq", "head"), P()),
        check_vma=False,
    )
```

```python
import math

import jax
import jax.numpy as jnp
from jax import lax
from jax.experimental import pallas as pl
from jax.experimental.pallas import tpu as pltpu
from jax.sharding import PartitionSpec as P

MESH = pl.DeviceIdType.MESH
BF = jnp.bfloat16
F32 = jnp.float32
HEAD_DIM = 72
TF = 32
P_SIZE = 512
W = 288
N = 128
SCALE = HEAD_DIM ** (-0.5)
GRAD_SCALE = 1.0 / math.sqrt(TF * P_SIZE)


def iota(shape, dim):
    return lax.broadcasted_iota(jnp.int32, shape, dim)


def onehot(cond):
    return jnp.where(cond, 1.0, 0.0).astype(BF)


def mm(a, b):
    return jnp.dot(a, b, preferred_element_type=F32)


def mm_nt(a, b):
    return lax.dot_general(a, b, (((1,), (1,)), ((), ())), preferred_element_type=F32)


def mm_tn(a, b):
    return lax.dot_general(a, b, (((0,), (0,)), ((), ())), preferred_element_type=F32)


def masks():
    own = onehot(iota((N, N), 1) // 32 == iota((N, N), 0) % 4)
    fold = onehot(iota((N, 32), 0) % 32 == iota((N, 32), 1))
    return own, fold


def target(c, n, rows):
    b, j, p = c // 32, (c % 32) // 4, c % 4
    return j * rows + jnp.where(b < 2 * n, 4 * b + p, 6 * n + b)


def packing(n, rows):
    return onehot(iota((8 * rows, 96 * n), 0) == target(iota((1, 96 * n), 1), n, rows))


def unpacking(n, rows):
    return onehot(iota((96 * n, 8 * rows), 1) == target(iota((96 * n, 1), 0), n, rows))


def pack(arrays, rows, sel, own, fold, dst):
    tails = [mm_nt(x[:, 256:W], fold).astype(BF) * own for x in arrays]
    for g in range(4):
        at = slice(32 * g, 32 * g + 32)
        stack = [x[at, N * t : N * t + N] for x in arrays for t in range(2)] + [x[at] for x in tails]
        dst[8 * g : 8 * g + 8] = mm(sel, jnp.concatenate(stack, axis=0)).astype(BF).reshape(8, rows, N)


def unpack(src, n, rows, sel, own, fold):
    parts = [mm(sel, src[8 * g : 8 * g + 8].reshape(8 * rows, N)).astype(BF) for g in range(4)]

    def tile(b):
        return jnp.concatenate([p[32 * b : 32 * b + 32] for p in parts], axis=0)

    return [
        jnp.concatenate([tile(2 * a), tile(2 * a + 1), mm(tile(2 * n + a) * own, fold).astype(BF)], axis=1)
        for a in range(n)
    ]


def kernel(
    q_hbm, k_hbm, v_hbm, g_hbm, w_hbm, s_hbm,
    grads_out, proj_out, gate_out,
    q_in, k_in, v_in, g_in, w_in, s_in,
    g_send, g_recv, send, recv, back, home, grads, gates, gate_row,
    w4, s4, og_all, rs_a, rs_b, c_a, c_b, plane_a, plane_b, got_a, got_b,
    z_send, z_recv, z_sum, gate_send, gate_plane, gate_line,
    in_sem, s_sem, r_sem,
):
    i = lax.axis_index("seq")
    h = lax.axis_index("head")
    f = i // 4
    r = i % 4
    core = i % 2
    y = (i // 2) % 4
    x = (i // 8) % 4
    z = i // 32
    xy = x * 4 + y

    loads = []
    for n, (src, dst) in enumerate(
        ((g_hbm, g_in), (q_hbm, q_in), (k_hbm, k_in), (v_hbm, v_in), (w_hbm, w_in), (s_hbm, s_in))
    ):
        copy = pltpu.make_async_copy(src, dst, in_sem.at[n])
        copy.start()
        loads.append(copy)

    barrier = pltpu.get_barrier_semaphore()

    def greet(seq, head):
        pl.semaphore_signal(barrier, inc=1, device_id=(seq, head), device_id_type=MESH)

    greet(i, (h + 1) % 4)
    greet(i, (h + 3) % 4)

    def greet_frames(t, carry):
        greet(4 * ((f + t) % 32) + r, h)
        return carry

    lax.fori_loop(1, 32, greet_frames, 0)

    def greet_plane(t, carry):
        greet(((z * 4 + t // 2) * 4 + 2 * (t % 2) + 1 - y % 2) * 2 + core, h)
        return carry

    lax.fori_loop(0, 8, greet_plane, 0)
    greet(i + 1 - 2 * core, h)

    def greet_other_core(t, carry):
        greet((z * 16 + (xy + t) % 16) * 2 + 1 - core, h)
        return carry

    lax.fori_loop(1, 16, greet_other_core, 0)

    own, fold = masks()
    eye = onehot(iota((N, N), 0) == iota((N, N), 1))

    def scatter(src, dst, n):
        pltpu.make_async_copy(src.at[f], dst.at[f], r_sem.at[n]).start()

        def one(t, carry):
            j = (f + t) % 32
            pltpu.make_async_remote_copy(
                src.at[j], dst.at[f], s_sem.at[n], r_sem.at[n],
                device_id=(4 * j + r, h), device_id_type=MESH,
            ).start()
            return carry

        lax.fori_loop(1, 32, one, 0)

    def wait_all(ref, sem):
        pltpu.make_async_copy(ref, ref, sem).wait()

    loads[0].wait()
    pack([mm_nt(eye, g_in[...]).astype(BF)], 16, packing(1, 16), own, fold, g_send)
    pl.semaphore_wait(barrier, 57)
    scatter(g_send, g_recv, 14)
    for copy in loads[1:4]:
        copy.wait()
    to_rows, from_rows = packing(3, 32), unpacking(3, 32)
    pack([mm_nt(eye, ref[...]).astype(BF) for ref in (q_in, k_in, v_in)], 32, to_rows, own, fold, send)
    scatter(send, recv, 0)

    heads = [onehot(iota((1, W), 1) // HEAD_DIM == k) for k in range(4)]
    same = iota((N, N), 0) % 4 == iota((N, N), 1) % 4
    drow, dcol = iota((W, W), 0), iota((W, W), 1)
    dest = jnp.where(drow < 256, drow // 8, drow - 256)
    spread = onehot(dcol == dest % 16 * 18 + dest // 16 * 9 + jnp.where(drow < 256, drow % 8, 8))
    erow, ecol = iota((256, 192), 0), iota((256, 192), 1)
    ninths = onehot(ecol == erow % 8 * 32 + erow // 8)

    crow, ccol = iota((72, N), 0), iota((72, N), 1)
    squeeze = onehot(
        ccol == jnp.where(crow < 64, (crow % 32) // 4 * 16 + crow // 32 * 4 + crow % 4, (crow - 64) * 16 + 8)
    )
    repeat = onehot(iota((N, 32), 0) // 4 == iota((N, 32), 1))
    prow, pcol = iota((W, N), 0), iota((W, N), 1)
    place = [onehot(jnp.logical_and(pcol // 32 == k, prow == 256 + pcol - 32 * k)) for k in range(4)]

    wait_all(g_recv, r_sem.at[14])
    parts = [mm(squeeze, g_recv[8 * g : 8 * g + 8].reshape(N, N)).astype(BF) for g in range(4)]
    og_all[h] = jnp.concatenate(
        [p[0:32] for p in parts] + [p[32:64] for p in parts]
        + [jnp.concatenate([p[64:72] for p in parts], axis=0)],
        axis=0,
    )

    right, left = (h + 1) % 4, (h + 3) % 4
    first, second = pl.ds(0, 144), pl.ds(144, 144)

    def pass_on(slot, rows, peer, n):
        return pltpu.make_async_remote_copy(
            og_all.at[slot, rows], og_all.at[slot, rows], s_sem.at[n], r_sem.at[n],
            device_id=(i, peer), device_id_type=MESH,
        )

    ring = [
        pass_on(h, first, right, 5), pass_on(h, second, left, 6),
        pass_on(h, second, right, 7), pass_on(h, first, left, 8),
    ]
    for copy in ring:
        copy.start()

    loads[4].wait()
    loads[5].wait()
    for n in range(4):
        w4[n] = w_in[:, W * n : W * n + W]
        s4[n] = s_in[:, W * n : W * n + W]

    ring[0].wait_recv()
    far = [pass_on(left, first, right, 9)]
    far[0].start()
    ring[1].wait_recv()
    far.append(pass_on(right, second, left, 10))
    far[1].start()

    wait_all(recv, r_sem.at[0])
    q, k, v = unpack(recv, 3, 32, from_rows, own, fold)
    km = jnp.concatenate([k * m for m in heads], axis=0)
    vm = jnp.concatenate([v * m for m in heads], axis=0)
    scores = mm_nt(q, km) * SCALE
    probs = []
    for n in range(4):
        sc = jnp.where(same, scores[:, N * n : N * n + N], -1e30)
        e = jnp.where(same, jnp.exp(sc - jnp.max(sc, axis=-1, keepdims=True)), 0.0)
        probs.append(e / jnp.sum(e, axis=-1, keepdims=True))
    light = [p.astype(BF) for p in probs]
    out = mm(jnp.concatenate(light, axis=1), vm).astype(BF)
    out_at = [mm(out, m).astype(BF) for m in place]
    probs_t = [p.T for p in probs]
    light_t = [p.astype(BF) for p in probs_t]
    qm = jnp.concatenate([q * m for m in heads], axis=0)

    def shard(n, role):
        tail = mm(mm(repeat, og_all[n, 256:288]).astype(BF) * own, fold)
        up = jnp.concatenate([og_all[n, 0:128].astype(F32), og_all[n, 128:256].astype(F32), tail], axis=1)
        scaled = (up * s4[n]).astype(BF)
        wn = w4[n]
        gate_part = jnp.sum(up * mm(out, wn), axis=0, keepdims=True)
        scaled_t = mm_nt(spread, scaled).astype(BF)
        main = mm(scaled_t, out[:, :256])
        return mm_nt(scaled, wn), main, mm(scaled_t, out_at[role]), gate_part

    def tile(top, bottom):
        both = jnp.concatenate([top.reshape(32, 8, N), bottom.reshape(32, 8, N)], axis=1)
        return both.astype(BF).reshape(2, 16, 16, N)

    def place_ninths(parts):
        return mm(ninths[:, : 32 * len(parts)], jnp.concatenate(parts, axis=0).astype(BF))

    sibling = (i + 1 - 2 * core, h)

    def to_sibling(src, dst, n):
        copy = pltpu.make_async_remote_copy(
            src.at[:, 1 - core], dst, s_sem.at[n], r_sem.at[n], device_id=sibling, device_id_type=MESH
        )
        copy.start()
        return copy

    def to_plane(src, dst, n):
        pltpu.make_async_copy(src.at[:, xy], dst.at[xy], r_sem.at[n]).start()

        def one(t, carry):
            j = (xy + t) % 16
            pltpu.make_async_remote_copy(
                src.at[:, j], dst.at[xy], s_sem.at[n], r_sem.at[n],
                device_id=((z * 16 + j) * 2 + core, h), device_id_type=MESH,
            ).start()
            return carry

        lax.fori_loop(1, 16, one, 0)

    do, main, tail_acc, gate_part = shard(h, 0)
    gate_parts = [gate_part]
    rs_a[0] = tile(main[:256, :128], main[:256, 128:])
    extra = [main[256:, :128], main[256:, 128:]]
    ring[2].wait_recv()
    ring[3].wait_recv()
    for role, n in ((1, left), (2, right)):
        term, main, tail, gate_part = shard(n, role)
        gate_parts.append(gate_part)
        do += term
        tail_acc += tail
        rs_a[role] = tile(main[:256, :128], main[:256, 128:])
        extra += [main[256:, :128], main[256:, 128:]]
    rs_a[3] = tile(place_ninths(extra), jnp.zeros((256, N), F32))
    pair_a = to_sibling(rs_a, c_a, 1)
    pair_a.wait()
    plane_a[...] = (rs_a[:, core].astype(F32) + c_a[...].astype(F32)).astype(BF)
    to_plane(plane_a, got_a, 3)

    for copy in far:
        copy.wait_recv()
    term, main, tail, gate_part = shard((h + 2) % 4, 3)
    gate_parts.append(gate_part)
    tail_acc += tail
    rs_b[0] = tile(main[:256, :128], main[:256, 128:])
    rs_b[1] = tile(tail_acc[:256], place_ninths([tail_acc[256:], main[256:, :128], main[256:, 128:]]))
    pair_b = to_sibling(rs_b, c_b, 15)

    gate_send[...] = jnp.concatenate(
        [p[:, at] for p in gate_parts for at in (slice(0, 128), slice(128, 256))]
        + [jnp.concatenate([p[:, 256:W] for p in gate_parts], axis=1), jnp.zeros((7, N), F32)],
        axis=0,
    ).astype(BF)
    spot = i % 32
    pltpu.make_async_copy(gate_send, gate_plane.at[spot], r_sem.at[12]).start()

    def gate_to_plane(t, carry):
        pltpu.make_async_remote_copy(
            gate_send, gate_plane.at[spot], s_sem.at[12], r_sem.at[12],
            device_id=(z * 32 + (spot + t) % 32, h), device_id_type=MESH,
        ).start()
        return carry

    lax.fori_loop(1, 32, gate_to_plane, 0)

    do = (do + term).astype(BF)
    dprob, dprob_t = mm_nt(do, vm), mm_nt(vm, do)
    dlight, dlight_t = [], []
    for n in range(4):
        dp = dprob[:, N * n : N * n + N]
        delta = jnp.sum(light[n].astype(F32) * dp, axis=-1, keepdims=True)
        dlight.append((probs[n] * (dp - delta)).astype(BF))
        dp = dprob_t[N * n : N * n + N]
        delta = jnp.sum(light_t[n].astype(F32) * dp, axis=0, keepdims=True)
        dlight_t.append((probs_t[n] * (dp - delta)).astype(BF))

    pair_b.wait()
    plane_b[...] = (rs_b[:, core].astype(F32) + c_b[...].astype(F32)).astype(BF)
    to_plane(plane_b, got_b, 16)

    dq = (mm(jnp.concatenate(dlight, axis=1), km) * SCALE).astype(BF)
    dk = (mm(jnp.concatenate(dlight_t, axis=1), qm) * SCALE).astype(BF)
    dom = jnp.concatenate([do * m for m in heads], axis=0)
    dv = mm(jnp.concatenate(light_t, axis=1), dom).astype(BF)
    pack([dq, dk, dv], 32, to_rows, own, fold, back)
    scatter(back, home, 2)

    wait_all(gate_plane, r_sem.at[12])
    total = gate_plane[0].astype(F32)
    for n in range(1, 32):
        total += gate_plane[n].astype(F32)
    gate_line[...] = total.astype(BF)
    slot = h * 4 + z
    pltpu.make_async_copy(gate_line, gates.at[slot], r_sem.at[11]).start()

    def to_line(t, carry):
        j = (slot + t) % 16
        pltpu.make_async_remote_copy(
            gate_line, gates.at[slot], s_sem.at[11], r_sem.at[11],
            device_id=(j % 4 * 32 + i % 32, j // 4), device_id_type=MESH,
        ).start()
        return carry

    lax.fori_loop(1, 16, to_line, 0)

    wait_all(got_a, r_sem.at[3])
    sum_a = got_a[0].astype(F32)
    for n in range(1, 16):
        sum_a += got_a[n].astype(F32)
    wait_all(got_b, r_sem.at[16])
    sum_b = got_b[0].astype(F32)
    for n in range(1, 16):
        sum_b += got_b[n].astype(F32)
    tiles = [sum_a[0], sum_a[1], sum_a[2], sum_b[0]]
    ends = [(sum_a[3, 2 * n : 2 * n + 1], sum_a[3, 2 * n + 1 : 2 * n + 2]) for n in range(3)] + [(sum_b[1, 9:10], sum_b[1, 10:11])]
    tail = sum_b[1].astype(BF)
    pad = jnp.zeros((7, N), F32)
    for role, n in ((0, h), (1, left), (2, right), (3, (h + 2) % 4)):
        back_to_0 = onehot(jnp.logical_and(iota((N, N), 0) == 32 * role + iota((N, N), 1), iota((N, N), 1) < 32))
        lanes = [
            jnp.concatenate([tiles[role][8 * t : 8 * t + 8], ends[role][t], pad], axis=0) for t in range(2)
        ]
        z_send[n] = jnp.concatenate(lanes + [mm(tail, back_to_0)], axis=1).astype(BF)
    pltpu.make_async_copy(z_send.at[z], z_recv.at[z], r_sem.at[4]).start()
    for t in range(1, 4):
        j = (z + t) % 4
        pltpu.make_async_remote_copy(
            z_send.at[j], z_recv.at[z], s_sem.at[4], r_sem.at[4],
            device_id=(j * 32 + i % 32, h), device_id_type=MESH,
        ).start()
    wait_all(z_recv, r_sem.at[4])
    total = z_recv[0].astype(F32)
    for n in range(1, 4):
        total += z_recv[n].astype(F32)
    z_sum[...] = total[0:9, 0:W] * GRAD_SCALE
    stores = [pltpu.make_async_copy(z_sum, proj_out, in_sem.at[6])]
    stores[0].start()

    wait_all(home, r_sem.at[2])
    for n, grad in enumerate(unpack(home, 3, 32, from_rows, own, fold)):
        for t, at in enumerate((slice(0, 128), slice(128, 256), slice(256, W))):
            grads[n, at] = grad[:, at].astype(F32).T.astype(BF)
        stores.append(pltpu.make_async_copy(grads.at[n], grads_out.at[n], in_sem.at[n]))
        stores[-1].start()

    wait_all(gates, r_sem.at[11])
    rows = [[] for n in range(4)]
    for m in range(4):
        total = gates[4 * m].astype(F32)
        for n in range(1, 4):
            total += gates[4 * m + n].astype(F32)
        for role, n in enumerate((m, (m + 3) % 4, (m + 1) % 4, (m + 2) % 4)):
            rows[n].append(jnp.concatenate(
                [total[2 * role : 2 * role + 1], total[2 * role + 1 : 2 * role + 2], total[8:9, 32 * role : 32 * role + 32]], axis=1
            ))
    gate_row[...] = jnp.concatenate([a + b + c + d for a, b, c, d in rows], axis=1) * GRAD_SCALE
    stores.append(pltpu.make_async_copy(gate_row, gate_out, in_sem.at[7]))
    stores[-1].start()

    for copy in ring + far:
        copy.wait_send()
    wait_all(g_send.at[pl.ds(0, 31)], s_sem.at[14])
    wait_all(send.at[pl.ds(0, 31)], s_sem.at[0])
    wait_all(back.at[pl.ds(0, 31)], s_sem.at[2])
    wait_all(plane_a.at[:, pl.ds(0, 15)], s_sem.at[3])
    wait_all(plane_b.at[:, pl.ds(0, 15)], s_sem.at[16])
    wait_all(z_send.at[pl.ds(0, 3)], s_sem.at[4])
    wait_all(gates.at[pl.ds(0, 15)], s_sem.at[11])
    wait_all(gate_plane.at[pl.ds(0, 31)], s_sem.at[12])
    for copy in stores:
        copy.wait()


def finish(grads, proj_in, gate_in, dq_ref, dk_ref, dv_ref, proj_ref, gate_ref):
    dq_ref[...] = grads[0]
    dk_ref[...] = grads[1]
    dv_ref[...] = grads[2]
    proj_ref[...] = proj_in[...]
    gate_ref[...] = gate_in[...]


def body(queries, key_heads, value_heads, out_grad, out_proj, gate_scale):
    hbm = pl.BlockSpec(memory_space=pltpu.HBM)
    token = pltpu.VMEM((W, N), BF)
    home, proj, gate = pl.pallas_call(
        kernel,
        out_shape=(
            jax.ShapeDtypeStruct((3, W, N), BF),
            jax.ShapeDtypeStruct((9, W), F32),
            jax.ShapeDtypeStruct((1, 1152), F32),
        ),
        in_specs=[hbm] * 6,
        out_specs=(hbm,) * 3,
        scratch_shapes=[
            token, token, token, token,
            pltpu.VMEM((W, 1152), BF),
            pltpu.VMEM((1, 1152), F32),
            pltpu.VMEM((32, 16, N), BF),
            pltpu.VMEM((32, 16, N), BF),
            pltpu.VMEM((32, 32, N), BF),
            pltpu.VMEM((32, 32, N), BF),
            pltpu.VMEM((32, 32, N), BF),
            pltpu.VMEM((32, 32, N), BF),
            pltpu.VMEM((3, W, N), BF),
            pltpu.VMEM((16, 16, N), BF),
            pltpu.VMEM((1, 1152), F32),
            pltpu.VMEM((4, W, W), BF),
            pltpu.VMEM((4, 1, W), F32),
            pltpu.VMEM((4, W, N), BF),
            pltpu.VMEM((4, 2, 16, 16, N), BF),
            pltpu.VMEM((2, 2, 16, 16, N), BF),
            pltpu.VMEM((4, 16, 16, N), BF),
            pltpu.VMEM((2, 16, 16, N), BF),
            pltpu.VMEM((4, 16, 16, N), BF),
            pltpu.VMEM((2, 16, 16, N), BF),
            pltpu.VMEM((16, 4, 16, N), BF),
            pltpu.VMEM((16, 2, 16, N), BF),
            pltpu.VMEM((4, 16, 384), BF),
            pltpu.VMEM((4, 16, 384), BF),
            pltpu.VMEM((9, W), F32),
            pltpu.VMEM((16, N), BF),
            pltpu.VMEM((32, 16, N), BF),
            pltpu.VMEM((16, N), BF),
            pltpu.SemaphoreType.DMA((8,)),
            pltpu.SemaphoreType.DMA((17,)),
            pltpu.SemaphoreType.DMA((17,)),
        ],
        compiler_params=pltpu.CompilerParams(
            collective_id=0, has_side_effects=True, vmem_limit_bytes=60 * 1024 * 1024
        ),
    )(queries.T, key_heads.T, value_heads.T, out_grad.T, out_proj.T, gate_scale)
    dq, dk, dv, proj, gate = pl.pallas_call(
        finish,
        out_shape=(
            jax.ShapeDtypeStruct((W, N), BF),
            jax.ShapeDtypeStruct((W, N), BF),
            jax.ShapeDtypeStruct((W, N), BF),
            jax.ShapeDtypeStruct((9, W), F32),
            jax.ShapeDtypeStruct((1, 1152), F32),
        ),
        in_specs=[pl.BlockSpec(memory_space=pltpu.VMEM)] * 3,
        out_specs=(pl.BlockSpec(memory_space=pltpu.VMEM),) * 5,
        compiler_params=pltpu.CompilerParams(vmem_limit_bytes=60 * 1024 * 1024),
    )(home, proj, gate)
    return dq.T, dk.T, dv.T, proj, gate


def solution(mesh):
    placed = (
        P("seq", "head"),
        P("seq", "head"),
        P("seq", "head"),
        P("seq", "head"),
        P(None, "head"),
        P(),
    )
    return jax.shard_map(
        body,
        mesh=mesh,
        in_specs=placed,
        out_specs=(P("seq", "head"), P("seq", "head"), P("seq", "head"), P("seq", "head"), P()),
        check_vma=False,
    )
```

```python
import math

import jax
import jax.numpy as jnp
from jax import lax
from jax.experimental import pallas as pl
from jax.experimental.pallas import tpu as pltpu
from jax.sharding import PartitionSpec as P

MESH = pl.DeviceIdType.MESH
BF = jnp.bfloat16
F32 = jnp.float32
HEAD_DIM = 72
TF = 32
P_SIZE = 512
W = 288
N = 128
SCALE = HEAD_DIM ** (-0.5)
GRAD_SCALE = 1.0 / math.sqrt(TF * P_SIZE)


def iota(shape, dim):
    return lax.broadcasted_iota(jnp.int32, shape, dim)


def onehot(cond):
    return jnp.where(cond, 1.0, 0.0).astype(BF)


def mm(a, b):
    return jnp.dot(a, b, preferred_element_type=F32)


def mm_nt(a, b):
    return lax.dot_general(a, b, (((1,), (1,)), ((), ())), preferred_element_type=F32)


def mm_tn(a, b):
    return lax.dot_general(a, b, (((0,), (0,)), ((), ())), preferred_element_type=F32)


def masks():
    own = onehot(iota((N, N), 1) // 32 == iota((N, N), 0) % 4)
    fold = onehot(iota((N, 32), 0) % 32 == iota((N, 32), 1))
    return own, fold


def target(c, n, rows):
    b, j, p = c // 32, (c % 32) // 4, c % 4
    return j * rows + jnp.where(b < 2 * n, 4 * b + p, 6 * n + b)


def packing(n, rows):
    return onehot(iota((8 * rows, 96 * n), 0) == target(iota((1, 96 * n), 1), n, rows))


def unpacking(n, rows):
    return onehot(iota((96 * n, 8 * rows), 1) == target(iota((96 * n, 1), 0), n, rows))


def pack(arrays, rows, sel, own, fold, dst):
    tails = [mm_nt(x[:, 256:W], fold).astype(BF) * own for x in arrays]
    for g in range(4):
        at = slice(32 * g, 32 * g + 32)
        stack = [x[at, N * t : N * t + N] for x in arrays for t in range(2)] + [x[at] for x in tails]
        dst[8 * g : 8 * g + 8] = mm(sel, jnp.concatenate(stack, axis=0)).astype(BF).reshape(8, rows, N)


def unpack(src, n, rows, sel, own, fold):
    parts = [mm(sel, src[8 * g : 8 * g + 8].reshape(8 * rows, N)).astype(BF) for g in range(4)]

    def tile(b):
        return jnp.concatenate([p[32 * b : 32 * b + 32] for p in parts], axis=0)

    return [
        jnp.concatenate([tile(2 * a), tile(2 * a + 1), mm(tile(2 * n + a) * own, fold).astype(BF)], axis=1)
        for a in range(n)
    ]


def kernel(
    q_hbm, k_hbm, v_hbm, g_hbm, w_hbm, s_hbm,
    grads_out, proj_out, gate_out,
    q_in, k_in, v_in, g_in, w_in, s_in,
    g_send, g_recv, send, recv, back, home, grads, gates, gate_row,
    w4, s4, og_all, rs_a, rs_b, c_a, c_b, plane_a, plane_b, got_a, got_b,
    z_send, z_recv, z_sum, gate_send, gate_plane, gate_line,
    in_sem, s_sem, r_sem,
):
    i = lax.axis_index("seq")
    h = lax.axis_index("head")
    f = i // 4
    r = i % 4
    core = i % 2
    y = (i // 2) % 4
    x = (i // 8) % 4
    z = i // 32
    xy = x * 4 + y

    loads = []
    for n, (src, dst) in enumerate(
        ((g_hbm, g_in), (q_hbm, q_in), (k_hbm, k_in), (v_hbm, v_in), (w_hbm, w_in), (s_hbm, s_in))
    ):
        copy = pltpu.make_async_copy(src, dst, in_sem.at[n])
        copy.start()
        loads.append(copy)

    barrier = pltpu.get_barrier_semaphore()

    def greet(seq, head):
        pl.semaphore_signal(barrier, inc=1, device_id=(seq, head), device_id_type=MESH)

    greet(i, (h + 1) % 4)
    greet(i, (h + 3) % 4)

    def greet_frames(t, carry):
        greet(4 * ((f + t) % 32) + r, h)
        return carry

    lax.fori_loop(1, 32, greet_frames, 0)

    def greet_plane(t, carry):
        greet(((z * 4 + t // 2) * 4 + 2 * (t % 2) + 1 - y % 2) * 2 + core, h)
        return carry

    lax.fori_loop(0, 8, greet_plane, 0)
    greet(i + 1 - 2 * core, h)

    def greet_other_core(t, carry):
        greet((z * 16 + (xy + t) % 16) * 2 + 1 - core, h)
        return carry

    lax.fori_loop(1, 16, greet_other_core, 0)

    own, fold = masks()
    eye = onehot(iota((N, N), 0) == iota((N, N), 1))

    def scatter(src, dst, n):
        pltpu.make_async_copy(src.at[f], dst.at[f], r_sem.at[n]).start()

        def one(t, carry):
            j = (z + 3 - t // 8) % 4 * 8 + (x + 3 - t % 8 // 2) % 4 * 2 + (y // 2 + 1 - t % 2) % 2
            pltpu.make_async_remote_copy(
                src.at[j], dst.at[f], s_sem.at[n], r_sem.at[n],
                device_id=(4 * j + r, h), device_id_type=MESH,
            ).start()
            return carry

        lax.fori_loop(0, 31, one, 0)

    def wait_all(ref, sem):
        pltpu.make_async_copy(ref, ref, sem).wait()

    loads[0].wait()
    pack([mm_nt(eye, g_in[...]).astype(BF)], 16, packing(1, 16), own, fold, g_send)
    pl.semaphore_wait(barrier, 57)
    scatter(g_send, g_recv, 14)
    for copy in loads[1:4]:
        copy.wait()
    to_rows, from_rows = packing(3, 32), unpacking(3, 32)
    pack([mm_nt(eye, ref[...]).astype(BF) for ref in (q_in, k_in, v_in)], 32, to_rows, own, fold, send)
    scatter(send, recv, 0)

    heads = [onehot(iota((1, W), 1) // HEAD_DIM == k) for k in range(4)]
    same = iota((N, N), 0) % 4 == iota((N, N), 1) % 4
    drow, dcol = iota((W, W), 0), iota((W, W), 1)
    dest = jnp.where(drow < 256, drow // 8, drow - 256)
    spread = onehot(dcol == dest % 16 * 18 + dest // 16 * 9 + jnp.where(drow < 256, drow % 8, 8))
    erow, ecol = iota((256, 192), 0), iota((256, 192), 1)
    ninths = onehot(ecol == erow % 8 * 32 + erow // 8)

    crow, ccol = iota((72, N), 0), iota((72, N), 1)
    squeeze = onehot(
        ccol == jnp.where(crow < 64, (crow % 32) // 4 * 16 + crow // 32 * 4 + crow % 4, (crow - 64) * 16 + 8)
    )
    repeat = onehot(iota((N, 32), 0) // 4 == iota((N, 32), 1))
    prow, pcol = iota((W, N), 0), iota((W, N), 1)
    place = [onehot(jnp.logical_and(pcol // 32 == k, prow == 256 + pcol - 32 * k)) for k in range(4)]

    wait_all(g_recv, r_sem.at[14])
    parts = [mm(squeeze, g_recv[8 * g : 8 * g + 8].reshape(N, N)).astype(BF) for g in range(4)]
    og_all[h] = jnp.concatenate(
        [p[0:32] for p in parts] + [p[32:64] for p in parts]
        + [jnp.concatenate([p[64:72] for p in parts], axis=0)],
        axis=0,
    )

    right, left = (h + 1) % 4, (h + 3) % 4
    first, second = pl.ds(0, 144), pl.ds(144, 144)

    def pass_on(slot, rows, peer, n):
        return pltpu.make_async_remote_copy(
            og_all.at[slot, rows], og_all.at[slot, rows], s_sem.at[n], r_sem.at[n],
            device_id=(i, peer), device_id_type=MESH,
        )

    ring = [
        pass_on(h, first, right, 5), pass_on(h, second, left, 6),
        pass_on(h, second, right, 7), pass_on(h, first, left, 8),
    ]
    for copy in ring:
        copy.start()

    loads[4].wait()
    loads[5].wait()
    for n in range(4):
        w4[n] = w_in[:, W * n : W * n + W]
        s4[n] = s_in[:, W * n : W * n + W]

    ring[0].wait_recv()
    far = [pass_on(left, first, right, 9)]
    far[0].start()
    ring[1].wait_recv()
    far.append(pass_on(right, second, left, 10))
    far[1].start()

    wait_all(recv, r_sem.at[0])
    q, k, v = unpack(recv, 3, 32, from_rows, own, fold)
    km = jnp.concatenate([k * m for m in heads], axis=0)
    vm = jnp.concatenate([v * m for m in heads], axis=0)
    scores = mm_nt(q, km) * SCALE
    probs = []
    for n in range(4):
        sc = jnp.where(same, scores[:, N * n : N * n + N], -1e30)
        e = jnp.where(same, jnp.exp(sc - jnp.max(sc, axis=-1, keepdims=True)), 0.0)
        probs.append(e / jnp.sum(e, axis=-1, keepdims=True))
    light = [p.astype(BF) for p in probs]
    out = mm(jnp.concatenate(light, axis=1), vm).astype(BF)
    out_at = [mm(out, m).astype(BF) for m in place]
    probs_t = [p.T for p in probs]
    light_t = [p.astype(BF) for p in probs_t]
    qm = jnp.concatenate([q * m for m in heads], axis=0)

    def shard(n, role):
        tail = mm(mm(repeat, og_all[n, 256:288]).astype(BF) * own, fold)
        up = jnp.concatenate([og_all[n, 0:128].astype(F32), og_all[n, 128:256].astype(F32), tail], axis=1)
        scaled = (up * s4[n]).astype(BF)
        wn = w4[n]
        gate_part = jnp.sum(up * mm(out, wn), axis=0, keepdims=True)
        scaled_t = mm_nt(spread, scaled).astype(BF)
        main = mm(scaled_t, out[:, :256])
        return mm_nt(scaled, wn), main, mm(scaled_t, out_at[role]), gate_part

    def tile(top, bottom):
        both = jnp.concatenate([top.reshape(32, 8, N), bottom.reshape(32, 8, N)], axis=1)
        return both.astype(BF).reshape(2, 16, 16, N)

    def place_ninths(parts):
        return mm(ninths[:, : 32 * len(parts)], jnp.concatenate(parts, axis=0).astype(BF))

    sibling = (i + 1 - 2 * core, h)

    def to_sibling(src, dst, n):
        copy = pltpu.make_async_remote_copy(
            src.at[:, 1 - core], dst, s_sem.at[n], r_sem.at[n], device_id=sibling, device_id_type=MESH
        )
        copy.start()
        return copy

    def to_plane(src, dst, n):
        pltpu.make_async_copy(src.at[:, xy], dst.at[xy], r_sem.at[n]).start()

        def one(t, carry):
            j = (x + 3 - t // 4) % 4 * 4 + (y + 3 - t % 4) % 4
            pltpu.make_async_remote_copy(
                src.at[:, j], dst.at[xy], s_sem.at[n], r_sem.at[n],
                device_id=((z * 16 + j) * 2 + core, h), device_id_type=MESH,
            ).start()
            return carry

        lax.fori_loop(0, 15, one, 0)

    do, main, tail_acc, gate_part = shard(h, 0)
    gate_parts = [gate_part]
    rs_a[0] = tile(main[:256, :128], main[:256, 128:])
    extra = [main[256:, :128], main[256:, 128:]]
    ring[2].wait_recv()
    ring[3].wait_recv()
    for role, n in ((1, left), (2, right)):
        term, main, tail, gate_part = shard(n, role)
        gate_parts.append(gate_part)
        do += term
        tail_acc += tail
        rs_a[role] = tile(main[:256, :128], main[:256, 128:])
        extra += [main[256:, :128], main[256:, 128:]]
    rs_a[3] = tile(place_ninths(extra), jnp.zeros((256, N), F32))
    pair_a = to_sibling(rs_a, c_a, 1)
    pair_a.wait()
    plane_a[...] = (rs_a[:, core].astype(F32) + c_a[...].astype(F32)).astype(BF)
    to_plane(plane_a, got_a, 3)

    for copy in far:
        copy.wait_recv()
    term, main, tail, gate_part = shard((h + 2) % 4, 3)
    gate_parts.append(gate_part)
    tail_acc += tail
    rs_b[0] = tile(main[:256, :128], main[:256, 128:])
    rs_b[1] = tile(tail_acc[:256], place_ninths([tail_acc[256:], main[256:, :128], main[256:, 128:]]))
    pair_b = to_sibling(rs_b, c_b, 15)

    gate_send[...] = jnp.concatenate(
        [p[:, at] for p in gate_parts for at in (slice(0, 128), slice(128, 256))]
        + [jnp.concatenate([p[:, 256:W] for p in gate_parts], axis=1), jnp.zeros((7, N), F32)],
        axis=0,
    ).astype(BF)
    spot = i % 32
    pltpu.make_async_copy(gate_send, gate_plane.at[spot], r_sem.at[12]).start()

    def gate_to_plane(t, carry):
        pltpu.make_async_remote_copy(
            gate_send, gate_plane.at[spot], s_sem.at[12], r_sem.at[12],
            device_id=(z * 32 + (spot + t) % 32, h), device_id_type=MESH,
        ).start()
        return carry

    lax.fori_loop(1, 32, gate_to_plane, 0)

    do = (do + term).astype(BF)
    dprob, dprob_t = mm_nt(do, vm), mm_nt(vm, do)
    dlight, dlight_t = [], []
    for n in range(4):
        dp = dprob[:, N * n : N * n + N]
        delta = jnp.sum(light[n].astype(F32) * dp, axis=-1, keepdims=True)
        dlight.append((probs[n] * (dp - delta)).astype(BF))
        dp = dprob_t[N * n : N * n + N]
        delta = jnp.sum(light_t[n].astype(F32) * dp, axis=0, keepdims=True)
        dlight_t.append((probs_t[n] * (dp - delta)).astype(BF))

    pair_b.wait()
    plane_b[...] = (rs_b[:, core].astype(F32) + c_b[...].astype(F32)).astype(BF)
    to_plane(plane_b, got_b, 16)

    dq = (mm(jnp.concatenate(dlight, axis=1), km) * SCALE).astype(BF)
    dk = (mm(jnp.concatenate(dlight_t, axis=1), qm) * SCALE).astype(BF)
    dom = jnp.concatenate([do * m for m in heads], axis=0)
    dv = mm(jnp.concatenate(light_t, axis=1), dom).astype(BF)
    pack([dq, dk, dv], 32, to_rows, own, fold, back)
    scatter(back, home, 2)

    wait_all(gate_plane, r_sem.at[12])
    total = gate_plane[0].astype(F32)
    for n in range(1, 32):
        total += gate_plane[n].astype(F32)
    gate_line[...] = total.astype(BF)
    slot = h * 4 + z
    pltpu.make_async_copy(gate_line, gates.at[slot], r_sem.at[11]).start()

    def to_line(t, carry):
        j = (h + 3 - t // 4) % 4 * 4 + (z + 3 - t % 4) % 4
        pltpu.make_async_remote_copy(
            gate_line, gates.at[slot], s_sem.at[11], r_sem.at[11],
            device_id=(j % 4 * 32 + i % 32, j // 4), device_id_type=MESH,
        ).start()
        return carry

    lax.fori_loop(0, 15, to_line, 0)

    wait_all(got_a, r_sem.at[3])
    sum_a = got_a[0].astype(F32)
    for n in range(1, 16):
        sum_a += got_a[n].astype(F32)
    wait_all(got_b, r_sem.at[16])
    sum_b = got_b[0].astype(F32)
    for n in range(1, 16):
        sum_b += got_b[n].astype(F32)
    tiles = [sum_a[0], sum_a[1], sum_a[2], sum_b[0]]
    ends = [(sum_a[3, 2 * n : 2 * n + 1], sum_a[3, 2 * n + 1 : 2 * n + 2]) for n in range(3)] + [(sum_b[1, 9:10], sum_b[1, 10:11])]
    tail = sum_b[1].astype(BF)
    pad = jnp.zeros((7, N), F32)
    for role, n in ((0, h), (1, left), (2, right), (3, (h + 2) % 4)):
        back_to_0 = onehot(jnp.logical_and(iota((N, N), 0) == 32 * role + iota((N, N), 1), iota((N, N), 1) < 32))
        lanes = [
            jnp.concatenate([tiles[role][8 * t : 8 * t + 8], ends[role][t], pad], axis=0) for t in range(2)
        ]
        z_send[n] = jnp.concatenate(lanes + [mm(tail, back_to_0)], axis=1).astype(BF)
    pltpu.make_async_copy(z_send.at[z], z_recv.at[z], r_sem.at[4]).start()
    for t in range(1, 4):
        j = (z + t) % 4
        pltpu.make_async_remote_copy(
            z_send.at[j], z_recv.at[z], s_sem.at[4], r_sem.at[4],
            device_id=(j * 32 + i % 32, h), device_id_type=MESH,
        ).start()
    wait_all(z_recv, r_sem.at[4])
    total = z_recv[0].astype(F32)
    for n in range(1, 4):
        total += z_recv[n].astype(F32)
    z_sum[...] = total[0:9, 0:W] * GRAD_SCALE
    stores = [pltpu.make_async_copy(z_sum, proj_out, in_sem.at[6])]
    stores[0].start()

    wait_all(home, r_sem.at[2])
    for n, grad in enumerate(unpack(home, 3, 32, from_rows, own, fold)):
        for t, at in enumerate((slice(0, 128), slice(128, 256), slice(256, W))):
            grads[n, at] = grad[:, at].astype(F32).T.astype(BF)
        stores.append(pltpu.make_async_copy(grads.at[n], grads_out.at[n], in_sem.at[n]))
        stores[-1].start()

    wait_all(gates, r_sem.at[11])
    rows = [[] for n in range(4)]
    for m in range(4):
        total = gates[4 * m].astype(F32)
        for n in range(1, 4):
            total += gates[4 * m + n].astype(F32)
        for role, n in enumerate((m, (m + 3) % 4, (m + 1) % 4, (m + 2) % 4)):
            rows[n].append(jnp.concatenate(
                [total[2 * role : 2 * role + 1], total[2 * role + 1 : 2 * role + 2], total[8:9, 32 * role : 32 * role + 32]], axis=1
            ))
    gate_row[...] = jnp.concatenate([a + b + c + d for a, b, c, d in rows], axis=1) * GRAD_SCALE
    stores.append(pltpu.make_async_copy(gate_row, gate_out, in_sem.at[7]))
    stores[-1].start()

    for copy in ring + far:
        copy.wait_send()
    wait_all(g_send.at[pl.ds(0, 31)], s_sem.at[14])
    wait_all(send.at[pl.ds(0, 31)], s_sem.at[0])
    wait_all(back.at[pl.ds(0, 31)], s_sem.at[2])
    wait_all(plane_a.at[:, pl.ds(0, 15)], s_sem.at[3])
    wait_all(plane_b.at[:, pl.ds(0, 15)], s_sem.at[16])
    wait_all(z_send.at[pl.ds(0, 3)], s_sem.at[4])
    wait_all(gates.at[pl.ds(0, 15)], s_sem.at[11])
    wait_all(gate_plane.at[pl.ds(0, 31)], s_sem.at[12])
    for copy in stores:
        copy.wait()


def finish(grads, proj_in, gate_in, dq_ref, dk_ref, dv_ref, proj_ref, gate_ref):
    dq_ref[...] = grads[0]
    dk_ref[...] = grads[1]
    dv_ref[...] = grads[2]
    proj_ref[...] = proj_in[...]
    gate_ref[...] = gate_in[...]


def body(queries, key_heads, value_heads, out_grad, out_proj, gate_scale):
    hbm = pl.BlockSpec(memory_space=pltpu.HBM)
    token = pltpu.VMEM((W, N), BF)
    home, proj, gate = pl.pallas_call(
        kernel,
        out_shape=(
            jax.ShapeDtypeStruct((3, W, N), BF),
            jax.ShapeDtypeStruct((9, W), F32),
            jax.ShapeDtypeStruct((1, 1152), F32),
        ),
        in_specs=[hbm] * 6,
        out_specs=(hbm,) * 3,
        scratch_shapes=[
            token, token, token, token,
            pltpu.VMEM((W, 1152), BF),
            pltpu.VMEM((1, 1152), F32),
            pltpu.VMEM((32, 16, N), BF),
            pltpu.VMEM((32, 16, N), BF),
            pltpu.VMEM((32, 32, N), BF),
            pltpu.VMEM((32, 32, N), BF),
            pltpu.VMEM((32, 32, N), BF),
            pltpu.VMEM((32, 32, N), BF),
            pltpu.VMEM((3, W, N), BF),
            pltpu.VMEM((16, 16, N), BF),
            pltpu.VMEM((1, 1152), F32),
            pltpu.VMEM((4, W, W), BF),
            pltpu.VMEM((4, 1, W), F32),
            pltpu.VMEM((4, W, N), BF),
            pltpu.VMEM((4, 2, 16, 16, N), BF),
            pltpu.VMEM((2, 2, 16, 16, N), BF),
            pltpu.VMEM((4, 16, 16, N), BF),
            pltpu.VMEM((2, 16, 16, N), BF),
            pltpu.VMEM((4, 16, 16, N), BF),
            pltpu.VMEM((2, 16, 16, N), BF),
            pltpu.VMEM((16, 4, 16, N), BF),
            pltpu.VMEM((16, 2, 16, N), BF),
            pltpu.VMEM((4, 16, 384), BF),
            pltpu.VMEM((4, 16, 384), BF),
            pltpu.VMEM((9, W), F32),
            pltpu.VMEM((16, N), BF),
            pltpu.VMEM((32, 16, N), BF),
            pltpu.VMEM((16, N), BF),
            pltpu.SemaphoreType.DMA((8,)),
            pltpu.SemaphoreType.DMA((17,)),
            pltpu.SemaphoreType.DMA((17,)),
        ],
        compiler_params=pltpu.CompilerParams(
            collective_id=0, has_side_effects=True, vmem_limit_bytes=60 * 1024 * 1024
        ),
    )(queries.T, key_heads.T, value_heads.T, out_grad.T, out_proj.T, gate_scale)
    dq, dk, dv, proj, gate = pl.pallas_call(
        finish,
        out_shape=(
            jax.ShapeDtypeStruct((W, N), BF),
            jax.ShapeDtypeStruct((W, N), BF),
            jax.ShapeDtypeStruct((W, N), BF),
            jax.ShapeDtypeStruct((9, W), F32),
            jax.ShapeDtypeStruct((1, 1152), F32),
        ),
        in_specs=[pl.BlockSpec(memory_space=pltpu.VMEM)] * 3,
        out_specs=(pl.BlockSpec(memory_space=pltpu.VMEM),) * 5,
        compiler_params=pltpu.CompilerParams(vmem_limit_bytes=60 * 1024 * 1024),
    )(home, proj, gate)
    return dq.T, dk.T, dv.T, proj, gate


def solution(mesh):
    placed = (
        P("seq", "head"),
        P("seq", "head"),
        P("seq", "head"),
        P("seq", "head"),
        P(None, "head"),
        P(),
    )
    return jax.shard_map(
        body,
        mesh=mesh,
        in_specs=placed,
        out_specs=(P("seq", "head"), P("seq", "head"), P("seq", "head"), P("seq", "head"), P()),
        check_vma=False,
    )
```

```python
import math

import jax
import jax.numpy as jnp
from jax import lax
from jax.experimental import pallas as pl
from jax.experimental.pallas import tpu as pltpu
from jax.sharding import PartitionSpec as P

MESH = pl.DeviceIdType.MESH
BF = jnp.bfloat16
F32 = jnp.float32
HEAD_DIM = 72
TF = 32
P_SIZE = 512
W = 288
N = 128
SCALE = HEAD_DIM ** (-0.5)
GRAD_SCALE = 1.0 / math.sqrt(TF * P_SIZE)


def iota(shape, dim):
    return lax.broadcasted_iota(jnp.int32, shape, dim)


def onehot(cond):
    return jnp.where(cond, 1.0, 0.0).astype(BF)


def mm(a, b):
    return jnp.dot(a, b, preferred_element_type=F32)


def mm_nt(a, b):
    return lax.dot_general(a, b, (((1,), (1,)), ((), ())), preferred_element_type=F32)


def mm_tn(a, b):
    return lax.dot_general(a, b, (((0,), (0,)), ((), ())), preferred_element_type=F32)


def masks():
    own = onehot(iota((N, N), 1) // 32 == iota((N, N), 0) % 4)
    fold = onehot(iota((N, 32), 0) % 32 == iota((N, 32), 1))
    return own, fold


def target(c, n, rows):
    b, j, p = c // 32, (c % 32) // 4, c % 4
    return j * rows + jnp.where(b < 2 * n, 4 * b + p, 6 * n + b)


def packing(n, rows):
    return onehot(iota((8 * rows, 96 * n), 0) == target(iota((1, 96 * n), 1), n, rows))


def unpacking(n, rows):
    return onehot(iota((96 * n, 8 * rows), 1) == target(iota((96 * n, 1), 0), n, rows))


def pack(arrays, rows, sel, own, fold, dst):
    tails = [mm_nt(x[:, 256:W], fold).astype(BF) * own for x in arrays]
    for g in range(4):
        at = slice(32 * g, 32 * g + 32)
        stack = [x[at, N * t : N * t + N] for x in arrays for t in range(2)] + [x[at] for x in tails]
        dst[8 * g : 8 * g + 8] = mm(sel, jnp.concatenate(stack, axis=0)).astype(BF).reshape(8, rows, N)


def unpack(src, n, rows, sel, own, fold):
    parts = [mm(sel, src[8 * g : 8 * g + 8].reshape(8 * rows, N)).astype(BF) for g in range(4)]

    def tile(b):
        return jnp.concatenate([p[32 * b : 32 * b + 32] for p in parts], axis=0)

    return [
        jnp.concatenate([tile(2 * a), tile(2 * a + 1), mm(tile(2 * n + a) * own, fold).astype(BF)], axis=1)
        for a in range(n)
    ]


def kernel(
    q_hbm, k_hbm, v_hbm, g_hbm, w_hbm, s_hbm,
    grads_out, proj_out, gate_out,
    q_in, k_in, v_in, g_in, w_in, s_in,
    g_send, g_recv, send, recv, back, home, grads, gates, gate_row,
    w4, s4, og_all, rs_a, rs_b, c_a, c_b, plane_a, plane_b, got_a, got_b,
    z_send, z_recv, z_sum, gate_line,
    in_sem, s_sem, r_sem,
):
    i = lax.axis_index("seq")
    h = lax.axis_index("head")
    f = i // 4
    r = i % 4
    core = i % 2
    y = (i // 2) % 4
    x = (i // 8) % 4
    z = i // 32
    xy = x * 4 + y

    loads = []
    for n, (src, dst) in enumerate(
        ((g_hbm, g_in), (q_hbm, q_in), (k_hbm, k_in), (v_hbm, v_in), (w_hbm, w_in), (s_hbm, s_in))
    ):
        copy = pltpu.make_async_copy(src, dst, in_sem.at[n])
        copy.start()
        loads.append(copy)

    barrier = pltpu.get_barrier_semaphore()

    def greet(seq, head):
        pl.semaphore_signal(barrier, inc=1, device_id=(seq, head), device_id_type=MESH)

    greet(i, (h + 1) % 4)
    greet(i, (h + 3) % 4)

    def greet_frames(t, carry):
        greet(4 * ((f + t) % 32) + r, h)
        return carry

    lax.fori_loop(1, 32, greet_frames, 0)

    def greet_plane(t, carry):
        greet(((z * 4 + t // 2) * 4 + 2 * (t % 2) + 1 - y % 2) * 2 + core, h)
        return carry

    lax.fori_loop(0, 8, greet_plane, 0)
    greet(i + 1 - 2 * core, h)

    own, fold = masks()
    eye = onehot(iota((N, N), 0) == iota((N, N), 1))

    def scatter(src, dst, n):
        pltpu.make_async_copy(src.at[f], dst.at[f], r_sem.at[n]).start()

        def one(t, carry):
            j = (z + 3 - t // 8) % 4 * 8 + (x + 3 - t % 8 // 2) % 4 * 2 + (y // 2 + 1 - t % 2) % 2
            pltpu.make_async_remote_copy(
                src.at[j], dst.at[f], s_sem.at[n], r_sem.at[n],
                device_id=(4 * j + r, h), device_id_type=MESH,
            ).start()
            return carry

        lax.fori_loop(0, 31, one, 0)

    def wait_all(ref, sem):
        pltpu.make_async_copy(ref, ref, sem).wait()

    loads[0].wait()
    pack([mm_nt(eye, g_in[...]).astype(BF)], 16, packing(1, 16), own, fold, g_send)
    pl.semaphore_wait(barrier, 42)
    scatter(g_send, g_recv, 14)
    for copy in loads[1:4]:
        copy.wait()
    to_rows, from_rows = packing(3, 32), unpacking(3, 32)
    pack([mm_nt(eye, ref[...]).astype(BF) for ref in (q_in, k_in, v_in)], 32, to_rows, own, fold, send)
    scatter(send, recv, 0)

    heads = [onehot(iota((1, W), 1) // HEAD_DIM == k) for k in range(4)]
    same = iota((N, N), 0) % 4 == iota((N, N), 1) % 4
    drow, dcol = iota((W, W), 0), iota((W, W), 1)
    dest = jnp.where(drow < 256, drow // 8, drow - 256)
    spread = onehot(dcol == dest % 16 * 18 + dest // 16 * 9 + jnp.where(drow < 256, drow % 8, 8))
    erow, ecol = iota((256, 192), 0), iota((256, 192), 1)
    ninths = onehot(ecol == erow % 8 * 32 + erow // 8)

    crow, ccol = iota((72, N), 0), iota((72, N), 1)
    squeeze = onehot(
        ccol == jnp.where(crow < 64, (crow % 32) // 4 * 16 + crow // 32 * 4 + crow % 4, (crow - 64) * 16 + 8)
    )
    repeat = onehot(iota((N, 32), 0) // 4 == iota((N, 32), 1))
    prow, pcol = iota((W, N), 0), iota((W, N), 1)
    place = [onehot(jnp.logical_and(pcol // 32 == k, prow == 256 + pcol - 32 * k)) for k in range(4)]

    wait_all(g_recv, r_sem.at[14])
    parts = [mm(squeeze, g_recv[8 * g : 8 * g + 8].reshape(N, N)).astype(BF) for g in range(4)]
    og_all[h] = jnp.concatenate(
        [p[0:32] for p in parts] + [p[32:64] for p in parts]
        + [jnp.concatenate([p[64:72] for p in parts], axis=0)],
        axis=0,
    )

    right, left = (h + 1) % 4, (h + 3) % 4
    first, second = pl.ds(0, 144), pl.ds(144, 144)

    def pass_on(slot, rows, peer, n):
        return pltpu.make_async_remote_copy(
            og_all.at[slot, rows], og_all.at[slot, rows], s_sem.at[n], r_sem.at[n],
            device_id=(i, peer), device_id_type=MESH,
        )

    ring = [
        pass_on(h, first, right, 5), pass_on(h, second, left, 6),
        pass_on(h, second, right, 7), pass_on(h, first, left, 8),
    ]
    for copy in ring:
        copy.start()

    loads[4].wait()
    loads[5].wait()
    for n in range(4):
        w4[n] = w_in[:, W * n : W * n + W]
        s4[n] = s_in[:, W * n : W * n + W]

    ring[0].wait_recv()
    far = [pass_on(left, first, right, 9)]
    far[0].start()
    ring[1].wait_recv()
    far.append(pass_on(right, second, left, 10))
    far[1].start()

    wait_all(recv, r_sem.at[0])
    q, k, v = unpack(recv, 3, 32, from_rows, own, fold)
    km = jnp.concatenate([k * m for m in heads], axis=0)
    vm = jnp.concatenate([v * m for m in heads], axis=0)
    scores = mm_nt(q, km) * SCALE
    probs = []
    for n in range(4):
        sc = jnp.where(same, scores[:, N * n : N * n + N], -1e30)
        e = jnp.where(same, jnp.exp(sc - jnp.max(sc, axis=-1, keepdims=True)), 0.0)
        probs.append(e / jnp.sum(e, axis=-1, keepdims=True))
    light = [p.astype(BF) for p in probs]
    out = mm(jnp.concatenate(light, axis=1), vm).astype(BF)
    out_at = [mm(out, m).astype(BF) for m in place]
    probs_t = [p.T for p in probs]
    light_t = [p.astype(BF) for p in probs_t]
    qm = jnp.concatenate([q * m for m in heads], axis=0)

    def shard(n, role):
        tail = mm(mm(repeat, og_all[n, 256:288]).astype(BF) * own, fold)
        up = jnp.concatenate([og_all[n, 0:128].astype(F32), og_all[n, 128:256].astype(F32), tail], axis=1)
        scaled = (up * s4[n]).astype(BF)
        wn = w4[n]
        gate_part = jnp.sum(up * mm(out, wn), axis=0, keepdims=True)
        scaled_t = mm_nt(spread, scaled).astype(BF)
        main = mm(scaled_t, out[:, :256])
        return mm_nt(scaled, wn), main, mm(scaled_t, out_at[role]), gate_part

    def tile(top, bottom):
        both = jnp.concatenate([top.reshape(32, 8, N), bottom.reshape(32, 8, N)], axis=1)
        return both.astype(BF).reshape(2, 16, 16, N)

    main_lanes = slice(0, 128), slice(128, 256)

    def to_all(rows):
        count = sum(r.shape[0] for r in rows)
        rows = rows + [jnp.zeros((8 - count, N), F32)] * (count < 8)
        block = jnp.concatenate(rows, axis=0)
        return jnp.concatenate([block] * 32, axis=0)

    def place_ninths(parts):
        return mm(ninths[:, : 32 * len(parts)], jnp.concatenate(parts, axis=0).astype(BF))

    sibling = (i + 1 - 2 * core, h)

    def to_sibling(src, dst, n):
        copy = pltpu.make_async_remote_copy(
            src.at[:, 1 - core], dst, s_sem.at[n], r_sem.at[n], device_id=sibling, device_id_type=MESH
        )
        copy.start()
        return copy

    def to_plane(src, dst, n):
        pltpu.make_async_copy(src.at[:, xy], dst.at[xy], r_sem.at[n]).start()

        def one(t, carry):
            j = (x + 3 - t // 4) % 4 * 4 + (y + 3 - t % 4) % 4
            pltpu.make_async_remote_copy(
                src.at[:, j], dst.at[xy], s_sem.at[n], r_sem.at[n],
                device_id=((z * 16 + j) * 2 + core, h), device_id_type=MESH,
            ).start()
            return carry

        lax.fori_loop(0, 15, one, 0)

    do, main, tail_acc, gate_part = shard(h, 0)
    gate_parts = [gate_part]
    rs_a[0] = tile(main[:256, :128], main[:256, 128:])
    extra = [main[256:, :128], main[256:, 128:]]
    ring[2].wait_recv()
    ring[3].wait_recv()
    for role, n in ((1, left), (2, right)):
        term, main, tail, gate_part = shard(n, role)
        gate_parts.append(gate_part)
        do += term
        tail_acc += tail
        rs_a[role] = tile(main[:256, :128], main[:256, 128:])
        extra += [main[256:, :128], main[256:, 128:]]
    rs_a[3] = tile(place_ninths(extra), to_all([p[:, at] for p in gate_parts for at in main_lanes]))
    pair_a = to_sibling(rs_a, c_a, 1)
    pair_a.wait()
    plane_a[...] = (rs_a[:, core].astype(F32) + c_a[...].astype(F32)).astype(BF)
    to_plane(plane_a, got_a, 3)

    for copy in far:
        copy.wait_recv()
    term, main, tail, gate_part = shard((h + 2) % 4, 3)
    gate_parts.append(gate_part)
    tail_acc += tail
    rs_b[0] = tile(main[:256, :128], main[:256, 128:])
    gate_tail = jnp.concatenate([p[:, 256:W] for p in gate_parts], axis=1)
    gate_rows = to_all([jnp.zeros((3, N), F32)] + [gate_part[:, at] for at in main_lanes] + [gate_tail, jnp.zeros((2, N), F32)])
    ninth = place_ninths([tail_acc[256:], main[256:, :128], main[256:, 128:]])
    rs_b[1] = tile(tail_acc[:256], ninth + gate_rows)
    pair_b = to_sibling(rs_b, c_b, 15)

    do = (do + term).astype(BF)
    dprob, dprob_t = mm_nt(do, vm), mm_nt(vm, do)
    dlight, dlight_t = [], []
    for n in range(4):
        dp = dprob[:, N * n : N * n + N]
        delta = jnp.sum(light[n].astype(F32) * dp, axis=-1, keepdims=True)
        dlight.append((probs[n] * (dp - delta)).astype(BF))
        dp = dprob_t[N * n : N * n + N]
        delta = jnp.sum(light_t[n].astype(F32) * dp, axis=0, keepdims=True)
        dlight_t.append((probs_t[n] * (dp - delta)).astype(BF))

    pair_b.wait()
    plane_b[...] = (rs_b[:, core].astype(F32) + c_b[...].astype(F32)).astype(BF)
    to_plane(plane_b, got_b, 16)

    dq = (mm(jnp.concatenate(dlight, axis=1), km) * SCALE).astype(BF)
    dk = (mm(jnp.concatenate(dlight_t, axis=1), qm) * SCALE).astype(BF)
    dom = jnp.concatenate([do * m for m in heads], axis=0)
    dv = mm(jnp.concatenate(light_t, axis=1), dom).astype(BF)
    pack([dq, dk, dv], 32, to_rows, own, fold, back)
    scatter(back, home, 2)

    wait_all(got_a, r_sem.at[3])
    sum_a = got_a[0].astype(F32)
    for n in range(1, 16):
        sum_a += got_a[n].astype(F32)
    wait_all(got_b, r_sem.at[16])
    sum_b = got_b[0].astype(F32)
    for n in range(1, 16):
        sum_b += got_b[n].astype(F32)
    gate_line[...] = jnp.concatenate(
        [sum_a[3, 8:14], sum_b[1, 11:14], jnp.zeros((7, N), F32)], axis=0
    ).astype(BF)
    slot = h * 4 + z
    pltpu.make_async_copy(gate_line, gates.at[slot], r_sem.at[11]).start()

    def to_line(t, carry):
        j = (h + 3 - t // 4) % 4 * 4 + (z + 3 - t % 4) % 4
        pltpu.make_async_remote_copy(
            gate_line, gates.at[slot], s_sem.at[11], r_sem.at[11],
            device_id=(j % 4 * 32 + i % 32, j // 4), device_id_type=MESH,
        ).start()
        return carry

    lax.fori_loop(0, 15, to_line, 0)

    tiles = [sum_a[0], sum_a[1], sum_a[2], sum_b[0]]
    ends = [(sum_a[3, 2 * n : 2 * n + 1], sum_a[3, 2 * n + 1 : 2 * n + 2]) for n in range(3)] + [(sum_b[1, 9:10], sum_b[1, 10:11])]
    tail = sum_b[1].astype(BF)
    pad = jnp.zeros((7, N), F32)
    for role, n in ((0, h), (1, left), (2, right), (3, (h + 2) % 4)):
        back_to_0 = onehot(jnp.logical_and(iota((N, N), 0) == 32 * role + iota((N, N), 1), iota((N, N), 1) < 32))
        lanes = [
            jnp.concatenate([tiles[role][8 * t : 8 * t + 8], ends[role][t], pad], axis=0) for t in range(2)
        ]
        z_send[n] = jnp.concatenate(lanes + [mm(tail, back_to_0)], axis=1).astype(BF)
    pltpu.make_async_copy(z_send.at[z], z_recv.at[z], r_sem.at[4]).start()
    for t in range(1, 4):
        j = (z + t) % 4
        pltpu.make_async_remote_copy(
            z_send.at[j], z_recv.at[z], s_sem.at[4], r_sem.at[4],
            device_id=(j * 32 + i % 32, h), device_id_type=MESH,
        ).start()
    wait_all(z_recv, r_sem.at[4])
    total = z_recv[0].astype(F32)
    for n in range(1, 4):
        total += z_recv[n].astype(F32)
    z_sum[...] = total[0:9, 0:W] * GRAD_SCALE
    stores = [pltpu.make_async_copy(z_sum, proj_out, in_sem.at[6])]
    stores[0].start()

    wait_all(home, r_sem.at[2])
    for n, grad in enumerate(unpack(home, 3, 32, from_rows, own, fold)):
        for t, at in enumerate((slice(0, 128), slice(128, 256), slice(256, W))):
            grads[n, at] = grad[:, at].astype(F32).T.astype(BF)
        stores.append(pltpu.make_async_copy(grads.at[n], grads_out.at[n], in_sem.at[n]))
        stores[-1].start()

    wait_all(gates, r_sem.at[11])
    rows = [[] for n in range(4)]
    for m in range(4):
        total = gates[4 * m].astype(F32)
        for n in range(1, 4):
            total += gates[4 * m + n].astype(F32)
        for role, n in enumerate((m, (m + 3) % 4, (m + 1) % 4, (m + 2) % 4)):
            rows[n].append(jnp.concatenate(
                [total[2 * role : 2 * role + 1], total[2 * role + 1 : 2 * role + 2], total[8:9, 32 * role : 32 * role + 32]], axis=1
            ))
    gate_row[...] = jnp.concatenate([a + b + c + d for a, b, c, d in rows], axis=1) * GRAD_SCALE
    stores.append(pltpu.make_async_copy(gate_row, gate_out, in_sem.at[7]))
    stores[-1].start()

    for copy in ring + far:
        copy.wait_send()
    wait_all(g_send.at[pl.ds(0, 31)], s_sem.at[14])
    wait_all(send.at[pl.ds(0, 31)], s_sem.at[0])
    wait_all(back.at[pl.ds(0, 31)], s_sem.at[2])
    wait_all(plane_a.at[:, pl.ds(0, 15)], s_sem.at[3])
    wait_all(plane_b.at[:, pl.ds(0, 15)], s_sem.at[16])
    wait_all(z_send.at[pl.ds(0, 3)], s_sem.at[4])
    wait_all(gates.at[pl.ds(0, 15)], s_sem.at[11])
    for copy in stores:
        copy.wait()


def finish(grads, proj_in, gate_in, dq_ref, dk_ref, dv_ref, proj_ref, gate_ref):
    dq_ref[...] = grads[0]
    dk_ref[...] = grads[1]
    dv_ref[...] = grads[2]
    proj_ref[...] = proj_in[...]
    gate_ref[...] = gate_in[...]


def body(queries, key_heads, value_heads, out_grad, out_proj, gate_scale):
    hbm = pl.BlockSpec(memory_space=pltpu.HBM)
    token = pltpu.VMEM((W, N), BF)
    home, proj, gate = pl.pallas_call(
        kernel,
        out_shape=(
            jax.ShapeDtypeStruct((3, W, N), BF),
            jax.ShapeDtypeStruct((9, W), F32),
            jax.ShapeDtypeStruct((1, 1152), F32),
        ),
        in_specs=[hbm] * 6,
        out_specs=(hbm,) * 3,
        scratch_shapes=[
            token, token, token, token,
            pltpu.VMEM((W, 1152), BF),
            pltpu.VMEM((1, 1152), F32),
            pltpu.VMEM((32, 16, N), BF),
            pltpu.VMEM((32, 16, N), BF),
            pltpu.VMEM((32, 32, N), BF),
            pltpu.VMEM((32, 32, N), BF),
            pltpu.VMEM((32, 32, N), BF),
            pltpu.VMEM((32, 32, N), BF),
            pltpu.VMEM((3, W, N), BF),
            pltpu.VMEM((16, 16, N), BF),
            pltpu.VMEM((1, 1152), F32),
            pltpu.VMEM((4, W, W), BF),
            pltpu.VMEM((4, 1, W), F32),
            pltpu.VMEM((4, W, N), BF),
            pltpu.VMEM((4, 2, 16, 16, N), BF),
            pltpu.VMEM((2, 2, 16, 16, N), BF),
            pltpu.VMEM((4, 16, 16, N), BF),
            pltpu.VMEM((2, 16, 16, N), BF),
            pltpu.VMEM((4, 16, 16, N), BF),
            pltpu.VMEM((2, 16, 16, N), BF),
            pltpu.VMEM((16, 4, 16, N), BF),
            pltpu.VMEM((16, 2, 16, N), BF),
            pltpu.VMEM((4, 16, 384), BF),
            pltpu.VMEM((4, 16, 384), BF),
            pltpu.VMEM((9, W), F32),
            pltpu.VMEM((16, N), BF),
            pltpu.SemaphoreType.DMA((8,)),
            pltpu.SemaphoreType.DMA((17,)),
            pltpu.SemaphoreType.DMA((17,)),
        ],
        compiler_params=pltpu.CompilerParams(
            collective_id=0, has_side_effects=True, vmem_limit_bytes=60 * 1024 * 1024
        ),
    )(queries.T, key_heads.T, value_heads.T, out_grad.T, out_proj.T, gate_scale)
    dq, dk, dv, proj, gate = pl.pallas_call(
        finish,
        out_shape=(
            jax.ShapeDtypeStruct((W, N), BF),
            jax.ShapeDtypeStruct((W, N), BF),
            jax.ShapeDtypeStruct((W, N), BF),
            jax.ShapeDtypeStruct((9, W), F32),
            jax.ShapeDtypeStruct((1, 1152), F32),
        ),
        in_specs=[pl.BlockSpec(memory_space=pltpu.VMEM)] * 3,
        out_specs=(pl.BlockSpec(memory_space=pltpu.VMEM),) * 5,
        compiler_params=pltpu.CompilerParams(vmem_limit_bytes=60 * 1024 * 1024),
    )(home, proj, gate)
    return dq.T, dk.T, dv.T, proj, gate


def solution(mesh):
    placed = (
        P("seq", "head"),
        P("seq", "head"),
        P("seq", "head"),
        P("seq", "head"),
        P(None, "head"),
        P(),
    )
    return jax.shard_map(
        body,
        mesh=mesh,
        in_specs=placed,
        out_specs=(P("seq", "head"), P("seq", "head"), P("seq", "head"), P("seq", "head"), P()),
        check_vma=False,
    )
```
